128 devices in a mesh: chan: 32 (over y, z, core), freq: 4 (over x).
Axes of the slice: x: 4, y: 4, z: 4, core: 2. Of those that a mesh axis runs over, the one named last changes fastest.
Arguments:
- records: bfloat16 [32768, 2, 8192], P('chan', None, 'freq'), may hold values from -400 to 400
- chan_pos: int32 [32768], replicated, may hold values from 0 to 511
- bin_row: int32 [512], replicated, may hold values from 0 to 511, each once
- pair_mask: int32 [32, 2], P('chan'), may hold values from 0 to 1, as said below
Outputs:
- traces: float32 [512, 1024], P('chan', 'freq')
The draws below stay inside these ranges and needn't reach their ends.
Inputs may be any that keep to these rules, and one draw needn't show every extreme that they name: `pair_mask`: 1 pairs receiver block i with virtual-source block i - j - 1; entries whose source block would be negative are ignored; the last receiver block pairs with all 2 of its sources.
All inputs are finite; a program needn't handle non-finite values.
Results may differ from the reference program's by a relative error of at most 0.0041.
Values may be sent and summed in bfloat16 or wider, within the bound.
No kernel may reach another device: no remote copies, remote signals or barrier semaphores. Data moves between devices by JAX's collectives and lax.ppermute only.
A program may use at most 192 MiB of HBM per device.

```python
import math
import jax
import jax.numpy as jnp
from jax import lax

CH = 1024
NF = 8192
LAGS = 1024
K = 512
REACH = 2
NB = 32
NCH = 32768


def draw_records(key, part):
    key = jax.random.fold_in(key, 11)
    key_a, key_b, key_c = jax.random.split(key, 3)
    chan_scale = jnp.exp(jax.random.uniform(key_a, (NCH, 1, 1), jnp.float32, 0.0, math.log(10.0)))
    ramp = jnp.exp(math.log(3.0) * jnp.arange(NF, dtype=jnp.float32) / (NF - 1))
    rough = jnp.exp(jax.random.uniform(key_b, (NCH, 1, NF), jnp.float32, -math.log(2.0), math.log(2.0)))
    values = jnp.clip(jax.random.normal(key_c, (NCH, 2, NF), jnp.float32), -6.0, 6.0)
    return (values * chan_scale * ramp[None, None, :] * rough).astype(jnp.bfloat16)


def draw_pair_mask(key, part):
    key = jax.random.fold_in(key, 13)
    coins = jax.random.randint(key, (NB, REACH), 0, 2, dtype=jnp.int32)
    last_row = jnp.arange(NB, dtype=jnp.int32)[:, None] == NB - 1
    return jnp.where(last_row, jnp.ones_like(coins), coins).astype(jnp.int32)


def set_ends(array, own_key, smallest, high):
    longest = array.shape.index(max(array.shape))
    spots = []
    for shift in (0, 1):
        where = [jax.random.randint(jax.random.fold_in(own_key, axis), (), 0, length) for axis, length in enumerate(array.shape)]
        where[longest] = (where[longest] + shift) % array.shape[longest]
        spots.append(tuple(where))
    return array.at[spots[0]].set(smallest).at[spots[1]].set(high)


def setup_inputs(seed: int = 0) -> dict:
    seeds = jax.random.split(jax.random.key(seed), 5)
    return {
        "records": draw_records(jax.random.fold_in(seeds[4], 71), 0),
        "chan_pos": set_ends(jax.random.randint(seeds[1], (NCH,), 0, K), jax.random.fold_in(seeds[1], 1), 0, K - 1).astype(jnp.int32),
        "bin_row": jax.random.permutation(seeds[2], K).astype(jnp.int32),
        "pair_mask": draw_pair_mask(jax.random.fold_in(seeds[4], 71), 0),
    }


water = 0.5
tiny = 1e-06

def lag_table(first, count):
    freqs = first + jnp.arange(count, dtype=jnp.int32)
    lagvec = jnp.arange(LAGS, dtype=jnp.int32) - LAGS // 2
    phase = jnp.mod(freqs[:, None] * lagvec[None, :], 2 * NF)
    theta = 2.0 * math.pi / (2 * NF) * phase.astype(jnp.float32)
    scale = 1.0 / math.sqrt(NF)
    return jnp.concatenate([jnp.cos(theta) * scale, -jnp.sin(theta) * scale], axis=0)

def reference(records, chan_pos, bin_row, pair_mask):
    rec = records.astype(jnp.float32)
    power = rec[:, 0] * rec[:, 0] + rec[:, 1] * rec[:, 1]
    level = water * lax.optimization_barrier(jnp.sum(power, axis=1)) / NF + tiny
    whitened = (rec / (power + level[:, None])[:, None, :]).astype(jnp.bfloat16)
    wblocks = whitened.reshape(NB, CH, 2, NF)
    rblocks = records.reshape(NB, CH, 2, NF)
    pblocks = chan_pos.reshape(NB, CH)

    def one_block(block, stack):
        own = rblocks[block].astype(jnp.float32)
        for step in range(REACH):
            source = block - step - 1
            valid = (source >= 0).astype(jnp.float32)
            safe = jnp.maximum(source, 0)
            wsrc = lax.dynamic_index_in_dim(wblocks, safe, 0, keepdims=False).astype(jnp.float32)
            psrc = lax.dynamic_index_in_dim(pblocks, safe, 0, keepdims=False)
            prod_re = own[:, 0] * wsrc[:, 0] + own[:, 1] * wsrc[:, 1]
            prod_im = own[:, 1] * wsrc[:, 0] - own[:, 0] * wsrc[:, 1]
            prods = jnp.stack([prod_re, prod_im], axis=1).astype(jnp.bfloat16).astype(jnp.float32)
            weight = valid * pair_mask[block, step].astype(jnp.float32)
            offset = jnp.abs(pblocks[block] - psrc)
            rows = bin_row[offset]
            stack = stack + jax.ops.segment_sum(prods * weight, rows, num_segments=K)
        return stack
    stack = lax.fori_loop(0, NB, one_block, jnp.zeros((K, 2, NF), jnp.float32))
    table = lag_table(0, NF)
    return jnp.dot(stack.reshape(K, 2 * NF), table, precision=lax.Precision.HIGHEST)
```

```python
import functools
import math

import jax
import jax.numpy as jnp
import numpy as np
from jax import lax
from jax.experimental import pallas as pl
from jax.experimental.pallas import tpu as pltpu
from jax.sharding import PartitionSpec as P

NF = 8192
LAGS = 1024

water = 0.5
tiny = 1e-06

TILE = 256
SLAB = 16
FINE = 16
CUTS = (1024, 512, 512)
VMEM = 40 * 1024 * 1024


def chips_along(block, distance):
    devices = range(lax.axis_size("chan"))
    route = [(i, i + 2 * distance) for i in devices if i + 2 * distance in devices]
    return lax.ppermute(block, "chan", route)


def to_sibling(block):
    return lax.ppermute(block, "chan", [(i, i ^ 1) for i in range(lax.axis_size("chan"))])


def phases(freqs, scale):
    lagvec = jnp.arange(LAGS, dtype=jnp.int32) - LAGS // 2
    phase = jnp.mod(freqs[:, None] * lagvec[None, :], 2 * NF)
    theta = 2.0 * math.pi / (2 * NF) * phase.astype(jnp.float32)
    return jnp.cos(theta) * scale, jnp.sin(theta) * scale


def split(value):
    high = value.astype(jnp.bfloat16)
    return high, (value - high.astype(jnp.float32)).astype(jnp.bfloat16)


def table_kernel(c1_ref, s1_ref, c2_ref, s2_ref, hi_ref, lo_ref):
    for a in range(TILE // FINE):
        c1, s1 = c1_ref[a : a + 1, :], s1_ref[a : a + 1, :]
        c2, s2 = c2_ref[...], s2_ref[...]
        for part, value in ((0, c1 * c2 - s1 * s2), (1, -(s1 * c2 + c1 * s2))):
            rows = pl.ds(part * TILE + a * FINE, FINE)
            hi_ref[0, rows, :], lo_ref[0, rows, :] = split(value)


def lag_tables(first, band):
    tiles = band // TILE
    coarse = first + FINE * jnp.arange(band // FINE, dtype=jnp.int32)
    c1, s1 = phases(coarse, 1.0 / math.sqrt(NF))
    c2, s2 = phases(jnp.arange(FINE, dtype=jnp.int32), 1.0)
    rows = pl.BlockSpec((TILE // FINE, LAGS), lambda t: (t, 0))
    fixed = pl.BlockSpec((FINE, LAGS), lambda t: (0, 0))
    out = pl.BlockSpec((1, 2 * TILE, LAGS), lambda t: (t, 0, 0))
    shape = jax.ShapeDtypeStruct((tiles, 2 * TILE, LAGS), jnp.bfloat16)
    return pl.pallas_call(
        table_kernel,
        grid=(tiles,),
        in_specs=[rows, rows, fixed, fixed],
        out_specs=[out, out],
        out_shape=[shape, shape],
        compiler_params=pltpu.CompilerParams(vmem_limit_bytes=VMEM),
        cost_estimate=pl.CostEstimate(
            flops=8 * band * LAGS, bytes_accessed=8 * band * LAGS, transcendentals=0
        ),
        name="lag_tables",
    )(c1, s1, c2, s2)


def load(ref, rows):
    return ref[0, rows, :].astype(jnp.float32), ref[1, rows, :].astype(jnp.float32)


def whiten(spectrum, level):
    re, im = spectrum
    inverse = 1.0 / (re * re + im * im + level)
    return (
        (re * inverse).astype(jnp.bfloat16).astype(jnp.float32),
        (im * inverse).astype(jnp.bfloat16).astype(jnp.float32),
    )


def put_product(prods, row, receiver, source):
    rre, rim = receiver
    wre, wim = source
    rows = pl.ds(row, SLAB)
    prods[rows, :TILE] = (rre * wre + rim * wim).astype(jnp.bfloat16)
    prods[rows, TILE:] = (rim * wre - rre * wim).astype(jnp.bfloat16)


def fill_onehot(onehot, target_ref):
    bins, pairs = onehot.shape
    for k in range(0, pairs, 256):
        row = lax.broadcasted_iota(jnp.int32, (bins, 256), 0)
        hit = row == target_ref[:, k : k + 256]
        onehot[:, k : k + 256] = jnp.where(hit, 1.0, 0.0).astype(jnp.bfloat16)


def local_kernel(role, target_ref, own, sib, own_level, sib_level, out_ref, onehot, prods):
    width = own.shape[1]

    @pl.when(pl.program_id(0) == 0)
    def _():
        fill_onehot(onehot, target_ref)

    def pairs(receiver, source, level):
        @pl.loop(0, width // SLAB)
        def _(s):
            row = pl.multiple_of(s * SLAB, SLAB)
            rows = pl.ds(row, SLAB)
            white = whiten(load(source, rows), level[rows, :])
            put_product(prods, row, load(receiver, rows), white)

    pl.when(role[0] == 0)(lambda: pairs(sib, own, own_level))
    pl.when(role[0] != 0)(lambda: pairs(own, sib, sib_level))
    out_ref[0] = jnp.dot(onehot[...], prods[...], preferred_element_type=jnp.float32)


def add_pairs(role, target_ref, prev, nxt, own, sib, prev_level, own_level, sib_level, onehot, prods):
    quarter = prev.shape[1]

    @pl.when(pl.program_id(0) == 0)
    def _():
        fill_onehot(onehot, target_ref)

    def pairs(l0, l1, l0_level, l1_level, odd):
        @pl.loop(0, quarter // SLAB)
        def _(s):
            row = pl.multiple_of(s * SLAB, SLAB)
            front = pl.ds(row, SLAB)
            back = pl.ds(quarter + row, SLAB)
            white = whiten(load(prev, front), prev_level[front, :])
            put_product(prods, row, load(l0, front), white)
            if odd:
                put_product(prods, 2 * quarter + row, load(l1, front), white)
            receiver = load(nxt, front)
            white = whiten(load(l1, back), l1_level[back, :])
            put_product(prods, quarter + row, receiver, white)
            if not odd:
                white = whiten(load(l0, back), l0_level[back, :])
                put_product(prods, 2 * quarter + row, receiver, white)

    for core in (0, 1):
        for odd in (0, 1):
            blocks = (own, sib, own_level, sib_level)
            if core:
                blocks = (sib, own, sib_level, own_level)
            run = functools.partial(pairs, *blocks, odd)
            pl.when((role[0] == core) & (role[1] == odd))(run)
    return jnp.dot(onehot[...], prods[...], preferred_element_type=jnp.float32)


def first_kernel(*refs):
    *ins, base, out_ref, onehot, prods = refs
    out_ref[0] = base[0] + add_pairs(*ins, onehot, prods)


def second_kernel(is_first, is_last, *refs):
    refs = list(refs)
    ins, refs = refs[:9], refs[9:]
    base, hi_ref, lo_ref, *refs = refs
    total_in = None if is_first else refs.pop(0)
    out_ref, onehot, prods, *refs = refs
    total = refs[0] if is_last else out_ref
    step = pl.program_id(0)
    stack = base[0] + add_pairs(*ins, onehot, prods)
    high, low = split(stack)
    lagged = jnp.dot(high, hi_ref[0], preferred_element_type=jnp.float32)
    lagged += jnp.dot(low, hi_ref[0], preferred_element_type=jnp.float32)
    lagged += jnp.dot(high, lo_ref[0], preferred_element_type=jnp.float32)

    @pl.when(step == 0)
    def _():
        total[...] = lagged if is_first else total_in[...] + lagged

    @pl.when(step > 0)
    def _():
        total[...] += lagged

    if is_last:
        parts, rows, lags = out_ref.shape
        bands = total.shape[1] // lags

        @pl.when(step == pl.num_programs(0) - 1)
        def _():
            for part in range(parts):
                r, f = part // bands * rows, part % bands * lags
                out_ref[part] = total[r : r + rows, f : f + lags].astype(jnp.bfloat16)


def shards(records, chan_pos, bin_row, pair_mask):
    here = lax.axis_index("chan")
    core, chip = here % 2, here // 2
    width, _, band = records.shape
    half, quarter = width // 2, width // 4
    bins = bin_row.shape[0]
    tiles = band // TILE
    devices = lax.axis_size("chan") * lax.axis_size("freq")

    def piece(array, first, count):
        return lax.dynamic_slice_in_dim(array, first, count).transpose(1, 0, 2)

    own_front = piece(records, core * half, quarter)
    own_back = piece(records, core * half + quarter, quarter)
    prev_own = chips_along(own_front, 1)
    next_own = chips_along(own_back, -1)
    rest, _, _ = lax.optimization_barrier((records, own_front, own_back))
    sib = to_sibling(piece(rest, (1 - core) * half, half))
    own = jnp.concatenate([own_front, own_back], axis=1)

    prev_sib, next_sib = [], []
    start = 0
    for cut in CUTS:
        prev_sib.append(chips_along(sib[:, :quarter, start : start + cut], 1))
        next_sib.append(chips_along(sib[:, quarter:, start : start + cut], -1))
        start += cut

    masks = lax.all_gather(pair_mask, "chan", tiled=True)

    def power(block):
        rec = block.astype(jnp.float32)
        return jnp.sum(rec[0] * rec[0] + rec[1] * rec[1], axis=1)

    totals = lax.psum(jnp.stack([power(own), power(sib)]), "freq")
    prev_totals = chips_along(totals[:, :quarter], 1)

    def level(total):
        return (water * total / NF + tiny)[:, None]

    own_level, sib_level = level(totals[0]), level(totals[1])

    def positions(block, offset):
        block = jnp.clip(block, 0, lax.axis_size("chan") - 1)
        return lax.dynamic_slice_in_dim(
            chan_pos, block * width + core * half + offset, quarter
        )

    def target(receiver, source, offset):
        apart = jnp.abs(positions(receiver, offset) - positions(source, offset))
        row = jnp.clip(receiver, 0, lax.axis_size("chan") - 1)
        used = jnp.where(receiver - source == 1, masks[row, 0], masks[row, 1])
        valid = (source >= 0) & (receiver < lax.axis_size("chan")) & (used > 0)
        return apart, jnp.broadcast_to(valid, apart.shape)

    l0, l1 = 2 * chip, 2 * chip + 1

    def slots(odd):
        before, after = l0 - 2 + odd, l0 + 2 + odd
        third_receiver = jnp.where(odd == 1, l1, after)
        third_source = jnp.where(odd == 1, before, l0)
        third_offset = jnp.where(odd == 1, 0, quarter)
        return [
            target(l0, before, 0),
            target(after, l1, quarter),
            target(third_receiver, third_source, third_offset),
        ]

    wanted = [target(l1, l0, 0), target(l1, l0, quarter)] + slots(core) + slots(1 - core)
    apart = jnp.concatenate([w[0] for w in wanted])
    valid = jnp.concatenate([w[1] for w in wanted])
    bin_ids = jnp.arange(bins, dtype=jnp.int32)
    row = jnp.sum(jnp.where(apart[:, None] == bin_ids[None, :], bin_row[None, :], 0), axis=1)
    row = jnp.where(valid, row, -1)[None, :]
    n = 3 * quarter
    local_row, own_row, sib_row = row[:, :half], row[:, half : half + n], row[:, half + n :]

    hi, lo = lag_tables(lax.axis_index("freq") * band, band)

    smem = pl.BlockSpec(memory_space=pltpu.SMEM)

    def whole(array):
        return pl.BlockSpec(array.shape, lambda t: (0,) * array.ndim)

    def columns(array, first=0):
        return pl.BlockSpec((2, array.shape[1], TILE), lambda t: (0, 0, t + first))

    def tile(array, first=0):
        return pl.BlockSpec((1, *array.shape[1:]), lambda t: (t + first, 0, 0))

    def params():
        return pltpu.CompilerParams(vmem_limit_bytes=VMEM)

    def scratch(count):
        return [
            pltpu.VMEM((bins, count), jnp.bfloat16),
            pltpu.VMEM((count, 2 * TILE), jnp.bfloat16),
        ]

    def cost(count, steps, lag=False):
        flops = steps * 2 * bins * 2 * TILE * (count + (3 * LAGS if lag else 0))
        return pl.CostEstimate(
            flops=flops, bytes_accessed=steps * 8 * bins * 2 * TILE, transcendentals=0
        )

    stack_shape = jax.ShapeDtypeStruct((tiles, bins, 2 * TILE), jnp.float32)
    roles = jnp.stack([core, core]).astype(jnp.int32)
    stack = pl.pallas_call(
        local_kernel,
        grid=(tiles,),
        in_specs=[smem, whole(local_row), columns(own), columns(sib)]
        + [whole(own_level), whole(sib_level)],
        out_specs=tile(stack_shape),
        out_shape=stack_shape,
        scratch_shapes=scratch(half),
        compiler_params=params(),
        cost_estimate=cost(half, tiles),
        name="local_pairs",
    )(roles, local_row, own, sib, own_level, sib_level)

    prev_level = level(prev_totals[0])
    stack = pl.pallas_call(
        first_kernel,
        grid=(tiles,),
        in_specs=[smem, whole(own_row), columns(prev_own), columns(next_own)]
        + [columns(own), columns(sib), whole(prev_level), whole(own_level)]
        + [whole(sib_level), tile(stack)],
        out_specs=tile(stack_shape),
        out_shape=stack_shape,
        scratch_shapes=scratch(n),
        compiler_params=params(),
        cost_estimate=cost(n, tiles),
        name="first_pairs",
    )(roles, own_row, prev_own, next_own, own, sib, prev_level, own_level, sib_level, stack)

    prev_level = level(prev_totals[1])
    roles = jnp.stack([core, 1 - core]).astype(jnp.int32)
    total = None
    start = 0
    for k, cut in enumerate(CUTS):
        is_first, is_last = k == 0, k == len(CUTS) - 1
        first, steps = start // TILE, cut // TILE
        ins = [roles, sib_row, prev_sib[k], next_sib[k], own, sib]
        ins += [prev_level, own_level, sib_level, stack, hi, lo]
        specs = [smem, whole(sib_row), columns(prev_sib[k]), columns(next_sib[k])]
        specs += [columns(own, first), columns(sib, first), whole(prev_level)]
        specs += [whole(own_level), whole(sib_level)]
        specs += [tile(stack, first), tile(hi, first), tile(lo, first)]
        if not is_first:
            ins.append(total)
            specs.append(whole(total))
        shape = jax.ShapeDtypeStruct((bins, LAGS), jnp.float32)
        extra = []
        if is_last:
            extra = [pltpu.VMEM(shape.shape, jnp.float32)]
            rows = bins // lax.axis_size("chan")
            lags = LAGS // lax.axis_size("freq")
            shape = jax.ShapeDtypeStruct((devices, rows, lags), jnp.bfloat16)
        total = pl.pallas_call(
            functools.partial(second_kernel, is_first, is_last),
            grid=(steps,),
            in_specs=specs,
            out_specs=whole(shape),
            out_shape=shape,
            scratch_shapes=scratch(n) + extra,
            compiler_params=params(),
            cost_estimate=cost(n, steps, True),
            name="second_pairs",
        )(*ins)
        start += cut

    parts = lax.all_to_all(total, ("chan", "freq"), 0, 0, tiled=True)
    return jnp.sum(parts.astype(jnp.float32), axis=0)


def solution(mesh):
    placed = (P("chan", None, "freq"), P(), P(), P("chan", None))
    return jax.shard_map(
        shards, mesh=mesh, in_specs=placed, out_specs=P("chan", "freq"), check_vma=False
    )
```

```python
import functools
import math

import jax
import jax.numpy as jnp
from jax import lax
from jax.experimental import pallas as pl
from jax.experimental.pallas import tpu as pltpu
from jax.sharding import PartitionSpec as P

NF = 8192
LAGS = 1024

water = 0.5
tiny = 1e-06

TILE = 256
SLAB = 16
FINE = 16
LANES = 128
PARTS = 4
CUTS = (768, 512, 512, 256)


def params(mebibytes=57):
    return pltpu.CompilerParams(vmem_limit_bytes=mebibytes * 1024 * 1024)


def cost():
    return pl.CostEstimate(flops=1, bytes_accessed=1, transcendentals=0)


def after(*arrays):
    return lax.optimization_barrier(arrays)


def to_sibling(block):
    return lax.ppermute(block, "chan", [(i, i ^ 1) for i in range(lax.axis_size("chan"))])


def to_chips(block, core_steps):
    devices = range(lax.axis_size("chan"))
    route = [(i, i + 2 * core_steps[i % 2]) for i in devices]
    return lax.ppermute(block, "chan", [(i, j) for i, j in route if j in devices])


def phases(first, tiles):
    tile = first + TILE * jnp.arange(tiles, dtype=jnp.int32)
    coarse = FINE * jnp.arange(TILE // FINE, dtype=jnp.int32)
    freqs = jnp.concatenate([tile, coarse, jnp.arange(FINE, dtype=jnp.int32)])
    lagvec = jnp.arange(LAGS, dtype=jnp.int32) - LAGS // 2
    phase = jnp.mod(freqs[:, None] * lagvec[None, :], 2 * NF)
    theta = 2.0 * math.pi / (2 * NF) * phase.astype(jnp.float32)
    scale = jnp.where(jnp.arange(len(freqs)) < tiles, 1.0 / math.sqrt(NF), 1.0)[:, None]
    return jnp.stack([jnp.cos(theta) * scale, -jnp.sin(theta) * scale], axis=1)


def turned(one, other):
    return one[0] * other[0] - one[1] * other[1], one[1] * other[0] + one[0] * other[1]


def planes_kernel(column, core_ref, *refs):
    count = (len(refs) - 4) // 2
    for n, records_ref in enumerate(refs[:2]):
        *planes_refs, power_ref = refs[2 + n * (count + 1) : 2 + (n + 1) * (count + 1)]
        channels, _, width = records_ref.shape
        width -= column
        for s in range(0, channels, SLAB):
            planes = jnp.swapaxes(records_ref[s : s + SLAB, :, column:], 0, 1)
            start = 0
            for ref in planes_refs:
                cut = ref.shape[2]
                ref[:, s : s + SLAB, :] = planes[:, :, start : start + cut]
                start += cut
            re, im = planes[0].astype(jnp.float32), planes[1].astype(jnp.float32)
            power = re * re + im * im
            total = power[:, :LANES]
            for f in range(LANES, width, LANES):
                total += power[:, f : f + LANES]
            power_ref[s : s + SLAB, :] = total


def planes(records, core, start, cuts):
    half = records.shape[0] // 2
    width = sum(cuts)
    loaded = width if start == 0 else records.shape[2]
    block = 128
    steps = half // block
    outs = [pl.BlockSpec((2, block, cut), lambda t, c: (0, t, 0)) for cut in cuts]
    outs += [pl.BlockSpec((block, LANES), lambda t, c: (t, 0))]
    shapes = [jax.ShapeDtypeStruct((2, half, cut), jnp.bfloat16) for cut in cuts]
    shapes += [jax.ShapeDtypeStruct((half, LANES), jnp.float32)]
    spec = pltpu.PrefetchScalarGridSpec(
        num_scalar_prefetch=1,
        grid=(steps,),
        in_specs=[
            pl.BlockSpec((block, 2, loaded), lambda t, c: (c[0] * steps + t, 0, 0)),
            pl.BlockSpec((block, 2, loaded), lambda t, c: ((1 - c[0]) * steps + t, 0, 0)),
        ],
        out_specs=outs * 2,
    )
    results = pl.pallas_call(
        functools.partial(planes_kernel, start),
        grid_spec=spec,
        out_shape=shapes * 2,
        compiler_params=params(),
        cost_estimate=cost(),
        name="planes",
    )(core, records, records)
    n = len(cuts)
    return list(results[:n]), results[n], list(results[n + 1 : -1]), results[-1]


def load(ref, rows):
    return ref[0, rows, :].astype(jnp.float32), ref[1, rows, :].astype(jnp.float32)


def whiten(spectrum, level):
    re, im = spectrum
    inverse = pltpu.reciprocal(re * re + im * im + level, approx=True)
    return (
        (re * inverse).astype(jnp.bfloat16).astype(jnp.float32),
        (im * inverse).astype(jnp.bfloat16).astype(jnp.float32),
    )


def pairs_kernel(is_first, is_last, core, row_ref, own, sib, from_own, from_sib, *refs):
    levels, tile_ref, coarse_ref, fine_ref, *refs = refs
    total_in = None if is_first else refs.pop(0)
    out_ref, onehot, table, *refs = refs
    total = refs.pop(0) if is_last else out_ref
    step = pl.program_id(0)
    count = own.shape[1] // len(refs)

    @pl.when(step == 0)
    def _():
        bins, pairs = onehot.shape
        for k in range(0, pairs, 256):
            bin_row = lax.broadcasted_iota(jnp.int32, (bins, 256), 0)
            hit = bin_row == row_ref[:, k : k + 256]
            onehot[:, k : k + 256] = jnp.where(hit, 1.0, 0.0).astype(jnp.bfloat16)

    def fill_table():
        coarse = turned(
            (tile_ref[0, 0:1, :], tile_ref[0, 1:2, :]), (coarse_ref[0], coarse_ref[1])
        )
        for a in range(TILE // FINE):
            rows = slice(a * FINE, (a + 1) * FINE)
            cos, sin = turned([part[a : a + 1, :] for part in coarse], (fine_ref[0], fine_ref[1]))
            table[rows, :] = cos.astype(jnp.bfloat16)
            table[TILE + a * FINE : TILE + (a + 1) * FINE, :] = sin.astype(jnp.bfloat16)

    def products(prods, start, even, odd, even_level, prev, after):
        for s in range(0, count, SLAB):
            rows = slice(start + s, start + s + SLAB)

            def put(slot, receiver, source):
                rre, rim = receiver
                wre, wim = source
                to = slice(slot * count + s, slot * count + s + SLAB)
                prods[to, :TILE] = (rre * wre + rim * wim).astype(jnp.bfloat16)
                prods[to, TILE:] = (rim * wre - rre * wim).astype(jnp.bfloat16)

            even_rec, odd_rec = load(even, rows), load(odd, rows)
            even_white = whiten(even_rec, levels[rows, even_level : even_level + 1])
            prev_white = whiten(load(prev, rows), levels[rows, 2:3])
            put(0, odd_rec, even_white)
            put(1, even_rec, prev_white)
            put(2, odd_rec, prev_white)
            put(3, load(after, rows), even_white)

    def run(*blocks):
        fill_table()
        stack = None
        for part, prods in enumerate(refs):
            products(prods, part * count, *blocks)
            pairs = slice(part * 4 * count, (part + 1) * 4 * count)
            sums = jnp.dot(onehot[:, pairs], prods[...], preferred_element_type=jnp.float32)
            stack = sums if stack is None else stack + sums
        high = stack.astype(jnp.bfloat16)
        low = (stack - high.astype(jnp.float32)).astype(jnp.bfloat16)
        lagged = jnp.dot(high, table[...], preferred_element_type=jnp.float32)
        lagged += jnp.dot(low, table[...], preferred_element_type=jnp.float32)

        @pl.when(step == 0)
        def _():
            total[...] = lagged if is_first else total_in[...] + lagged

        @pl.when(step > 0)
        def _():
            total[...] += lagged

    pl.when(core[0] == 0)(lambda: run(own, sib, 0, from_sib, from_own))
    pl.when(core[0] != 0)(lambda: run(sib, own, 1, from_own, from_sib))

    if is_last:
        parts, rows, lags = out_ref.shape
        bands = total.shape[1] // lags

        @pl.when(step == pl.num_programs(0) - 1)
        def _():
            for part in range(parts):
                r, f = part // bands * rows, part % bands * lags
                out_ref[part] = total[r : r + rows, f : f + lags].astype(jnp.bfloat16)


def add_pairs(first, core, row, own, sib, from_own, from_sib, levels, phase, total, out, bins):
    cut = own.shape[2]
    pairs = row.shape[1]
    by_tile, coarse, fine = phase

    def whole(array):
        return pl.BlockSpec(array.shape, lambda t: (0,) * array.ndim)

    def columns(array):
        return pl.BlockSpec((2, array.shape[1], TILE), lambda t: (0, 0, t))

    blocks = [own, sib, from_own, from_sib]
    ins = [core, row, *blocks, levels, by_tile, coarse, fine]
    specs = [pl.BlockSpec(memory_space=pltpu.SMEM), whole(row)]
    specs += [columns(b) for b in blocks] + [whole(levels)]
    specs += [pl.BlockSpec((1, 2, LAGS), lambda t: (t + first, 0, 0)), whole(coarse), whole(fine)]
    scratch = [pltpu.VMEM((bins, pairs), jnp.bfloat16), pltpu.VMEM((2 * TILE, LAGS), jnp.bfloat16)]
    if total is not None:
        ins.append(total)
        specs.append(whole(total))
    is_last = out is not None
    if is_last:
        scratch.append(pltpu.VMEM((bins, LAGS), jnp.float32))
    else:
        out = jax.ShapeDtypeStruct((bins, LAGS), jnp.float32)
    return pl.pallas_call(
        functools.partial(pairs_kernel, total is None, is_last),
        grid=(cut // TILE,),
        in_specs=specs,
        out_specs=whole(out),
        out_shape=out,
        scratch_shapes=scratch
        + [pltpu.VMEM((pairs // PARTS, 2 * TILE), jnp.bfloat16)] * PARTS,
        compiler_params=params(40),
        cost_estimate=cost(),
        name="add_pairs",
    )(*ins)


def shards(records, chan_pos, bin_row, pair_mask):
    here = lax.axis_index("chan")
    core, chip = here % 2, here // 2
    blocks, bands = lax.axis_size("chan"), lax.axis_size("freq")
    width, _, band = records.shape
    half = width // 2
    bins = bin_row.shape[0]

    core_ref = core.astype(jnp.int32)[None]
    own, own_power, give, give_power = planes(records, core_ref, 0, CUTS[:1])
    sib = [to_sibling(give[0])]
    moved = [to_chips(own[0], (-1, 1)), to_chips(sib[0], (1, -1))]
    records, sib[0] = after(records, sib[0])
    rest_own, more_own, rest, more_give = planes(records, core_ref, CUTS[0], CUTS[1:])
    own, own_power, give_power = own + rest_own, own_power + more_own, give_power + more_give

    totals = lax.psum(jnp.sum(jnp.stack([own_power, give_power]), axis=2), "freq")
    mask = pair_mask[0].astype(jnp.float32)
    own_info = jnp.concatenate([totals[0], mask])
    sib_info = to_sibling(jnp.concatenate([totals[1], mask]))
    own_info_moved = to_chips(own_info, (-1, 1))
    sib_info_moved = to_chips(sib_info, (1, -1))
    own[1], own_info_moved = after(own[1], own_info_moved)

    first, sib_info = after(lax.axis_index("freq") * band, sib_info)
    phase = phases(first, band // TILE)

    phase = phase[: band // TILE], *phase[band // TILE :].reshape(2, FINE, 2, LAGS).swapaxes(1, 2)

    sib += [to_sibling(block) for block in rest]
    sib[1], sib_info_moved, moved[1] = after(sib[1], sib_info_moved, moved[1])
    moved += [to_chips(own[1], (-1, 1)), to_chips(sib[1], (1, -1))]

    even_mask = jnp.where(core == 0, mask, sib_info[half:])
    odd_mask = jnp.where(core == 0, sib_info[half:], mask)
    prev_info = jnp.where(core == 0, sib_info_moved, own_info_moved)
    next_info = jnp.where(core == 0, own_info_moved, sib_info_moved)

    totals = jnp.stack([own_info[:half], sib_info[:half], prev_info[:half]], axis=1)
    levels = water * totals / NF + tiny

    places = jnp.pad(chan_pos.reshape(blocks, width), ((1, 1), (0, 0)))
    places = lax.dynamic_slice(places, (2 * chip, core * half), (4, half))
    prev_pos, even_pos, odd_pos, next_pos = places
    apart = jnp.abs(
        jnp.concatenate(
            [odd_pos - even_pos, even_pos - prev_pos, odd_pos - prev_pos, next_pos - even_pos]
        )
    )
    used = jnp.stack(
        [
            odd_mask[0] > 0,
            (even_mask[0] > 0) & (chip > 0),
            (odd_mask[1] > 0) & (chip > 0),
            (next_info[half + 1] > 0) & (chip < blocks // 2 - 1),
        ]
    )
    bin_ids = jnp.arange(bins, dtype=jnp.int32)
    row = jnp.sum(jnp.where(apart[:, None] == bin_ids[None, :], bin_row[None, :], 0), axis=1)
    row = jnp.where(jnp.repeat(used, half), row, -1)
    row = row.reshape(4, PARTS, half // PARTS).transpose(1, 0, 2).reshape(-1)

    out = jax.ShapeDtypeStruct((blocks * bands, bins // blocks, LAGS // bands), jnp.bfloat16)
    total, start = None, 0
    for k, cut in enumerate(CUTS):
        arrays = own[k], sib[k], moved[2 * k], moved[2 * k + 1]
        goal = out if k == len(CUTS) - 1 else None
        total = add_pairs(
            start // TILE, core_ref, row[None, :], *arrays, levels, phase, total, goal, bins
        )
        if k + 2 < len(CUTS):
            own[k + 2], sib[k + 2], total = after(own[k + 2], sib[k + 2], total)
            moved += [to_chips(own[k + 2], (-1, 1)), to_chips(sib[k + 2], (1, -1))]
        start += cut

    parts = lax.all_to_all(total, ("chan", "freq"), 0, 0, tiled=True)
    return jnp.sum(parts.astype(jnp.float32), axis=0)


def solution(mesh):
    placed = (P("chan", None, "freq"), P(), P(), P("chan", None))
    return jax.shard_map(
        shards, mesh=mesh, in_specs=placed, out_specs=P("chan", "freq"), check_vma=False
    )
```

```python
import functools
import math

import jax
import jax.numpy as jnp
from jax import lax
from jax.experimental import pallas as pl
from jax.experimental.pallas import tpu as pltpu
from jax.sharding import PartitionSpec as P

NF = 8192
LAGS = 1024

water = 0.5
tiny = 1e-06

TILE = 256
SLAB = 16
FINE = 16
LANES = 128
PARTS = 4
CUTS = (1024, 768, 256)


def params(mebibytes=57):
    return pltpu.CompilerParams(vmem_limit_bytes=mebibytes * 1024 * 1024)


def cost():
    return pl.CostEstimate(flops=1, bytes_accessed=1, transcendentals=0)


def after(*arrays):
    return lax.optimization_barrier(arrays)


def to_sibling(block):
    return lax.ppermute(block, "chan", [(i, i ^ 1) for i in range(lax.axis_size("chan"))])


def to_chips(block, core_steps, bands=0):
    devices, count = range(lax.axis_size("chan")), lax.axis_size("freq")
    route = [(i, i + 2 * core_steps[i % 2]) for i in devices]
    route = [(i, j) for i, j in route if j in devices]
    if not bands:
        return lax.ppermute(block, "chan", route)
    route = [
        (i * count + f, j * count + (f + bands) % count) for i, j in route for f in range(count)
    ]
    return lax.ppermute(block, ("chan", "freq"), route)


def phases(first, tiles):
    tile = first + TILE * jnp.arange(tiles, dtype=jnp.int32)
    coarse = FINE * jnp.arange(TILE // FINE, dtype=jnp.int32)
    freqs = jnp.concatenate([tile, coarse, jnp.arange(FINE, dtype=jnp.int32)])
    lagvec = jnp.arange(LAGS, dtype=jnp.int32) - LAGS // 2
    phase = jnp.mod(freqs[:, None] * lagvec[None, :], 2 * NF)
    theta = 2.0 * math.pi / (2 * NF) * phase.astype(jnp.float32)
    scale = jnp.where(jnp.arange(len(freqs)) < tiles, 1.0 / math.sqrt(NF), 1.0)[:, None]
    return jnp.cos(theta) * scale, -jnp.sin(theta) * scale


def turned(one, other):
    return one[0] * other[0] - one[1] * other[1], one[1] * other[0] + one[0] * other[1]


def planes_kernel(column, core_ref, *refs):
    count = (len(refs) - 4) // 2
    for n, records_ref in enumerate(refs[:2]):
        *planes_refs, power_ref = refs[2 + n * (count + 1) : 2 + (n + 1) * (count + 1)]
        channels, _, width = records_ref.shape
        width -= column
        for s in range(0, channels, SLAB):
            planes = jnp.swapaxes(records_ref[s : s + SLAB, :, column:], 0, 1)
            start = 0
            for ref in planes_refs:
                cut = ref.shape[2]
                ref[:, s : s + SLAB, :] = planes[:, :, start : start + cut]
                start += cut
            re, im = planes[0].astype(jnp.float32), planes[1].astype(jnp.float32)
            power = re * re + im * im
            total = power[:, :LANES]
            for f in range(LANES, width, LANES):
                total += power[:, f : f + LANES]
            power_ref[s : s + SLAB, :] = total


def planes(records, core, start, cuts):
    half = records.shape[0] // 2
    width = sum(cuts)
    loaded = width if start == 0 else records.shape[2]
    block = 128
    steps = half // block
    outs = [pl.BlockSpec((2, block, cut), lambda t, c: (0, t, 0)) for cut in cuts]
    outs += [pl.BlockSpec((block, LANES), lambda t, c: (t, 0))]
    shapes = [jax.ShapeDtypeStruct((2, half, cut), jnp.bfloat16) for cut in cuts]
    shapes += [jax.ShapeDtypeStruct((half, LANES), jnp.float32)]
    spec = pltpu.PrefetchScalarGridSpec(
        num_scalar_prefetch=1,
        grid=(steps,),
        in_specs=[
            pl.BlockSpec((block, 2, loaded), lambda t, c: (c[0] * steps + t, 0, 0)),
            pl.BlockSpec((block, 2, loaded), lambda t, c: ((1 - c[0]) * steps + t, 0, 0)),
        ],
        out_specs=outs * 2,
    )
    results = pl.pallas_call(
        functools.partial(planes_kernel, start),
        grid_spec=spec,
        out_shape=shapes * 2,
        compiler_params=params(),
        cost_estimate=cost(),
        name="planes",
    )(core, records, records)
    n = len(cuts)
    return list(results[:n]), results[n], list(results[n + 1 : -1]), results[-1]


def load(ref, rows):
    return ref[0, rows, :].astype(jnp.float32), ref[1, rows, :].astype(jnp.float32)


def whiten(spectrum, level):
    re, im = spectrum
    inverse = pltpu.reciprocal(re * re + im * im + level, approx=True)
    return (
        (re * inverse).astype(jnp.bfloat16).astype(jnp.float32),
        (im * inverse).astype(jnp.bfloat16).astype(jnp.float32),
    )


def pairs_kernel(first, is_last, core, row_ref, own, sib, from_own, from_sib, *refs):
    levels, cos_ref, sin_ref, *refs = refs
    total_in = refs.pop(0) if first else None
    out_ref, onehot, table, *refs = refs
    total = refs.pop(0) if is_last else out_ref
    step = pl.program_id(0)
    count = own.shape[1] // len(refs)

    @pl.when(step == 0)
    def _():
        bins, pairs = onehot.shape
        for k in range(0, pairs, 256):
            bin_row = lax.broadcasted_iota(jnp.int32, (bins, 256), 0)
            hit = bin_row == row_ref[:, k : k + 256]
            onehot[:, k : k + 256] = jnp.where(hit, 1.0, 0.0).astype(jnp.bfloat16)

    def fill_table():
        tiles = cos_ref.shape[0] - TILE // FINE - FINE
        start = pl.ds(first + step, 1)
        coarse, fine = slice(tiles, tiles + TILE // FINE), slice(tiles + TILE // FINE, None)
        turn = turned(
            (cos_ref[start, :], sin_ref[start, :]), (cos_ref[coarse, :], sin_ref[coarse, :])
        )
        steps = cos_ref[fine, :], sin_ref[fine, :]
        for a in range(TILE // FINE):
            rows = slice(a * FINE, (a + 1) * FINE)
            cos, sin = turned([part[a : a + 1, :] for part in turn], steps)
            table[rows, :] = cos.astype(jnp.bfloat16)
            table[TILE + a * FINE : TILE + (a + 1) * FINE, :] = sin.astype(jnp.bfloat16)

    def products(prods, start, even, odd, even_level, prev, after):
        for s in range(0, count, SLAB):
            rows = slice(start + s, start + s + SLAB)

            def put(slot, receiver, source):
                rre, rim = receiver
                wre, wim = source
                to = slice(slot * count + s, slot * count + s + SLAB)
                prods[to, :TILE] = (rre * wre + rim * wim).astype(jnp.bfloat16)
                prods[to, TILE:] = (rim * wre - rre * wim).astype(jnp.bfloat16)

            even_rec, odd_rec = load(even, rows), load(odd, rows)
            even_white = whiten(even_rec, levels[rows, even_level : even_level + 1])
            prev_white = whiten(load(prev, rows), levels[rows, 2:3])
            put(0, odd_rec, even_white)
            put(1, even_rec, prev_white)
            put(2, odd_rec, prev_white)
            put(3, load(after, rows), even_white)

    def run(*blocks):
        fill_table()
        stack = None
        for part, prods in enumerate(refs):
            products(prods, part * count, *blocks)
            pairs = slice(part * 4 * count, (part + 1) * 4 * count)
            sums = jnp.dot(onehot[:, pairs], prods[...], preferred_element_type=jnp.float32)
            stack = sums if stack is None else stack + sums
        high = stack.astype(jnp.bfloat16)
        low = (stack - high.astype(jnp.float32)).astype(jnp.bfloat16)
        lagged = jnp.dot(high, table[...], preferred_element_type=jnp.float32)
        lagged += jnp.dot(low, table[...], preferred_element_type=jnp.float32)

        @pl.when(step == 0)
        def _():
            total[...] = total_in[...] + lagged if first else lagged

        @pl.when(step > 0)
        def _():
            total[...] += lagged

    pl.when(core[0] == 0)(lambda: run(own, sib, 0, from_sib, from_own))
    pl.when(core[0] != 0)(lambda: run(sib, own, 1, from_own, from_sib))

    if is_last:
        parts, rows, lags = out_ref.shape
        bands = total.shape[1] // lags

        @pl.when(step == pl.num_programs(0) - 1)
        def _():
            for part in range(parts):
                r, f = part // bands * rows, part % bands * lags
                out_ref[part] = total[r : r + rows, f : f + lags].astype(jnp.bfloat16)


def add_pairs(first, core, row, own, sib, from_own, from_sib, levels, phase, total, out, bins):
    cut = own.shape[2]
    pairs = row.shape[1]

    def whole(array):
        return pl.BlockSpec(array.shape, lambda t: (0,) * array.ndim)

    def columns(array):
        return pl.BlockSpec((2, array.shape[1], TILE), lambda t: (0, 0, t))

    blocks = [own, sib, from_own, from_sib]
    ins = [core, row, *blocks, levels, *phase]
    specs = [pl.BlockSpec(memory_space=pltpu.SMEM), whole(row)]
    specs += [columns(b) for b in blocks] + [whole(levels)] + [whole(p) for p in phase]
    scratch = [pltpu.VMEM((bins, pairs), jnp.bfloat16), pltpu.VMEM((2 * TILE, LAGS), jnp.bfloat16)]
    if total is not None:
        ins.append(total)
        specs.append(whole(total))
    is_last = out is not None
    if is_last:
        scratch.append(pltpu.VMEM((bins, LAGS), jnp.float32))
    else:
        out = jax.ShapeDtypeStruct((bins, LAGS), jnp.float32)
    return pl.pallas_call(
        functools.partial(pairs_kernel, first, is_last),
        grid=(cut // TILE,),
        in_specs=specs,
        out_specs=whole(out),
        out_shape=out,
        scratch_shapes=scratch
        + [pltpu.VMEM((pairs // PARTS, 2 * TILE), jnp.bfloat16)] * PARTS,
        compiler_params=params(40),
        cost_estimate=cost(),
        name="add_pairs",
    )(*ins)


def shards(records, chan_pos, bin_row, pair_mask):
    here = lax.axis_index("chan")
    core, chip = here % 2, here // 2
    blocks, bands = lax.axis_size("chan"), lax.axis_size("freq")
    width, _, band = records.shape
    half = width // 2
    bins = bin_row.shape[0]

    core_ref = core.astype(jnp.int32)[None]
    own, own_power, give, give_power = planes(records, core_ref, 0, CUTS[:1])
    sib = [to_sibling(give[0])]
    moved = [to_chips(own[0], (-1, 1)), to_chips(sib[0], (1, -1))]
    records, sib[0] = after(records, sib[0])
    rest_own, more_own, rest, more_give = planes(records, core_ref, CUTS[0], CUTS[1:])
    own, own_power, give_power = own + rest_own, own_power + more_own, give_power + more_give

    totals = lax.psum(jnp.sum(jnp.stack([own_power, give_power]), axis=2), "freq")
    mask = pair_mask[0].astype(jnp.float32)
    own_info = jnp.concatenate([totals[0], mask])
    sib_info = to_sibling(jnp.concatenate([totals[1], mask]))
    own_info_moved = to_chips(own_info, (-1, 1), 1)
    sib_info_moved = to_chips(sib_info, (1, -1), 1)
    own[1], own_info_moved = after(own[1], own_info_moved)

    first, sib_info = after(lax.axis_index("freq") * band, sib_info)
    phase = phases(first, band // TILE)


    sib += [to_sibling(block) for block in rest]
    sib[1], sib_info_moved, moved[1] = after(sib[1], sib_info_moved, moved[1])
    moved += [to_chips(own[1], (-1, 1)), to_chips(sib[1], (1, -1))]

    even_mask = jnp.where(core == 0, mask, sib_info[half:])
    odd_mask = jnp.where(core == 0, sib_info[half:], mask)
    prev_info = jnp.where(core == 0, sib_info_moved, own_info_moved)
    next_info = jnp.where(core == 0, own_info_moved, sib_info_moved)

    totals = jnp.stack([own_info[:half], sib_info[:half], prev_info[:half]], axis=1)
    levels = water * totals / NF + tiny

    places = jnp.pad(chan_pos.reshape(blocks, width), ((1, 1), (0, 0)))
    places = lax.dynamic_slice(places, (2 * chip, core * half), (4, half))
    prev_pos, even_pos, odd_pos, next_pos = places
    apart = jnp.abs(
        jnp.concatenate(
            [odd_pos - even_pos, even_pos - prev_pos, odd_pos - prev_pos, next_pos - even_pos]
        )
    )
    used = jnp.stack(
        [
            odd_mask[0] > 0,
            (even_mask[0] > 0) & (chip > 0),
            (odd_mask[1] > 0) & (chip > 0),
            (next_info[half + 1] > 0) & (chip < blocks // 2 - 1),
        ]
    )
    bin_ids = jnp.arange(bins, dtype=jnp.int32)
    row = jnp.sum(jnp.where(apart[:, None] == bin_ids[None, :], bin_row[None, :], 0), axis=1)
    row = jnp.where(jnp.repeat(used, half), row, -1)
    row = row.reshape(4, PARTS, half // PARTS).transpose(1, 0, 2).reshape(-1)

    out = jax.ShapeDtypeStruct((blocks * bands, bins // blocks, LAGS // bands), jnp.bfloat16)
    total, start = None, 0
    for k, cut in enumerate(CUTS):
        arrays = own[k], sib[k], moved[2 * k], moved[2 * k + 1]
        goal = out if k == len(CUTS) - 1 else None
        total = add_pairs(
            start // TILE, core_ref, row[None, :], *arrays, levels, phase, total, goal, bins
        )
        if k + 2 < len(CUTS):
            own[k + 2], sib[k + 2], total = after(own[k + 2], sib[k + 2], total)
            moved += [to_chips(own[k + 2], (-1, 1)), to_chips(sib[k + 2], (1, -1))]
        start += cut

    parts = lax.all_to_all(total, ("chan", "freq"), 0, 0, tiled=True)
    return jnp.sum(parts.astype(jnp.float32), axis=0)


def solution(mesh):
    placed = (P("chan", None, "freq"), P(), P(), P("chan", None))
    return jax.shard_map(
        shards, mesh=mesh, in_specs=placed, out_specs=P("chan", "freq"), check_vma=False
    )
```

```python
import functools
import math

import jax
import jax.numpy as jnp
from jax import lax
from jax.experimental import pallas as pl
from jax.experimental.pallas import tpu as pltpu
from jax.sharding import PartitionSpec as P

NF = 8192
LAGS = 1024

water = 0.5
tiny = 1e-06

TILE = 256
SLAB = 16
FINE = 16
LANES = 128
PARTS = 4
CUTS = (1024, 768, 256)


def params(mebibytes=57):
    return pltpu.CompilerParams(vmem_limit_bytes=mebibytes * 1024 * 1024)


def cost():
    return pl.CostEstimate(flops=1, bytes_accessed=1, transcendentals=0)


def after(*arrays):
    return lax.optimization_barrier(arrays)


def to_sibling(block):
    return lax.ppermute(block, "chan", [(i, i ^ 1) for i in range(lax.axis_size("chan"))])


def to_chips(block, core_steps, bands=0):
    devices, count = range(lax.axis_size("chan")), lax.axis_size("freq")
    route = [(i, i + 2 * core_steps[i % 2]) for i in devices]
    route = [(i, j) for i, j in route if j in devices]
    if not bands:
        return lax.ppermute(block, "chan", route)
    route = [
        (i * count + f, j * count + (f + bands) % count) for i, j in route for f in range(count)
    ]
    return lax.ppermute(block, ("chan", "freq"), route)


def phases(first, tiles):
    tile = first + TILE * jnp.arange(tiles, dtype=jnp.int32)
    coarse = FINE * jnp.arange(TILE // FINE, dtype=jnp.int32)
    freqs = jnp.concatenate([tile, coarse, jnp.arange(FINE, dtype=jnp.int32)])
    lagvec = jnp.arange(LAGS, dtype=jnp.int32) - LAGS // 2
    phase = jnp.mod(freqs[:, None] * lagvec[None, :], 2 * NF)
    theta = 2.0 * math.pi / (2 * NF) * phase.astype(jnp.float32)
    scale = jnp.where(jnp.arange(len(freqs)) < tiles, 1.0 / math.sqrt(NF), 1.0)[:, None]
    return jnp.cos(theta) * scale, -jnp.sin(theta) * scale


def turned(one, other):
    return one[0] * other[0] - one[1] * other[1], one[1] * other[0] + one[0] * other[1]


def planes_kernel(column, core_ref, *refs):
    count = (len(refs) - 4) // 2
    for n, records_ref in enumerate(refs[:2]):
        *planes_refs, power_ref = refs[2 + n * (count + 1) : 2 + (n + 1) * (count + 1)]
        channels, _, width = records_ref.shape
        width -= column
        for s in range(0, channels, SLAB):
            planes = jnp.swapaxes(records_ref[s : s + SLAB, :, column:], 0, 1)
            start = 0
            for ref in planes_refs:
                cut = ref.shape[2]
                ref[:, s : s + SLAB, :] = planes[:, :, start : start + cut]
                start += cut
            re, im = planes[0].astype(jnp.float32), planes[1].astype(jnp.float32)
            power = re * re + im * im
            total = power[:, :LANES]
            for f in range(LANES, width, LANES):
                total += power[:, f : f + LANES]
            power_ref[s : s + SLAB, :] = total


def planes(records, core, start, cuts):
    half = records.shape[0] // 2
    width = sum(cuts)
    loaded = width if start == 0 else records.shape[2]
    block = 128
    steps = half // block
    outs = [pl.BlockSpec((2, block, cut), lambda t, c: (0, t, 0)) for cut in cuts]
    outs += [pl.BlockSpec((block, LANES), lambda t, c: (t, 0))]
    shapes = [jax.ShapeDtypeStruct((2, half, cut), jnp.bfloat16) for cut in cuts]
    shapes += [jax.ShapeDtypeStruct((half, LANES), jnp.float32)]
    spec = pltpu.PrefetchScalarGridSpec(
        num_scalar_prefetch=1,
        grid=(steps,),
        in_specs=[
            pl.BlockSpec((block, 2, loaded), lambda t, c: (c[0] * steps + t, 0, 0)),
            pl.BlockSpec((block, 2, loaded), lambda t, c: ((1 - c[0]) * steps + t, 0, 0)),
        ],
        out_specs=outs * 2,
    )
    results = pl.pallas_call(
        functools.partial(planes_kernel, start),
        grid_spec=spec,
        out_shape=shapes * 2,
        compiler_params=params(),
        cost_estimate=cost(),
        name="planes",
    )(core, records, records)
    n = len(cuts)
    return list(results[:n]), results[n], list(results[n + 1 : -1]), results[-1]


def load(ref, rows):
    return ref[0, rows, :].astype(jnp.float32), ref[1, rows, :].astype(jnp.float32)


def whiten(spectrum, level):
    re, im = spectrum
    inverse = pltpu.reciprocal(re * re + im * im + level, approx=True)
    return (
        (re * inverse).astype(jnp.bfloat16).astype(jnp.float32),
        (im * inverse).astype(jnp.bfloat16).astype(jnp.float32),
    )


def pairs_kernel(first, is_last, core, row_ref, own, sib, from_own, from_sib, *refs):
    levels, cos_ref, sin_ref, *refs = refs
    total_in = refs.pop(0) if first else None
    out_ref, *refs = refs
    give_ref = refs.pop(0) if is_last else None
    onehot, table, *refs = refs
    total = refs.pop(0) if is_last else out_ref
    step = pl.program_id(0)
    count = own.shape[1] // len(refs)

    @pl.when(step == 0)
    def _():
        bins, pairs = onehot.shape
        for k in range(0, pairs, 256):
            bin_row = lax.broadcasted_iota(jnp.int32, (bins, 256), 0)
            hit = bin_row == row_ref[:, k : k + 256]
            onehot[:, k : k + 256] = jnp.where(hit, 1.0, 0.0).astype(jnp.bfloat16)

    def fill_table():
        tiles = cos_ref.shape[0] - TILE // FINE - FINE
        start = pl.ds(first + step, 1)
        coarse, fine = slice(tiles, tiles + TILE // FINE), slice(tiles + TILE // FINE, None)
        turn = turned(
            (cos_ref[start, :], sin_ref[start, :]), (cos_ref[coarse, :], sin_ref[coarse, :])
        )
        steps = cos_ref[fine, :], sin_ref[fine, :]
        for a in range(TILE // FINE):
            rows = slice(a * FINE, (a + 1) * FINE)
            cos, sin = turned([part[a : a + 1, :] for part in turn], steps)
            table[rows, :] = cos.astype(jnp.bfloat16)
            table[TILE + a * FINE : TILE + (a + 1) * FINE, :] = sin.astype(jnp.bfloat16)

    def products(prods, start, even, odd, even_level, prev, after):
        for s in range(0, count, SLAB):
            rows = slice(start + s, start + s + SLAB)

            def put(slot, receiver, source):
                rre, rim = receiver
                wre, wim = source
                to = slice(slot * count + s, slot * count + s + SLAB)
                prods[to, :TILE] = (rre * wre + rim * wim).astype(jnp.bfloat16)
                prods[to, TILE:] = (rim * wre - rre * wim).astype(jnp.bfloat16)

            even_rec, odd_rec = load(even, rows), load(odd, rows)
            even_white = whiten(even_rec, levels[rows, even_level : even_level + 1])
            prev_white = whiten(load(prev, rows), levels[rows, 2:3])
            put(0, odd_rec, even_white)
            put(1, even_rec, prev_white)
            put(2, odd_rec, prev_white)
            put(3, load(after, rows), even_white)

    def run(*blocks):
        fill_table()
        stack = None
        for part, prods in enumerate(refs):
            products(prods, part * count, *blocks)
            pairs = slice(part * 4 * count, (part + 1) * 4 * count)
            sums = jnp.dot(onehot[:, pairs], prods[...], preferred_element_type=jnp.float32)
            stack = sums if stack is None else stack + sums
        stack = stack.astype(jnp.bfloat16)
        lagged = jnp.dot(stack, table[...], preferred_element_type=jnp.float32)

        @pl.when(step == 0)
        def _():
            total[...] = total_in[...] + lagged if first else lagged

        @pl.when(step > 0)
        def _():
            total[...] += lagged

    pl.when(core[0] == 0)(lambda: run(own, sib, 0, from_sib, from_own))
    pl.when(core[0] != 0)(lambda: run(sib, own, 1, from_own, from_sib))

    if is_last:
        parts, rows, lags = out_ref.shape
        bands = total.shape[1] // lags

        @pl.when(step == pl.num_programs(0) - 1)
        def _():
            for part in range(parts):
                chip, f = part // bands, part % bands * lags
                for ref, owner in ((out_ref, core[0]), (give_ref, 1 - core[0])):
                    start = pl.multiple_of((2 * chip + owner) * rows, rows)
                    ref[part] = total[pl.ds(start, rows), f : f + lags]


def add_pairs(first, core, row, own, sib, from_own, from_sib, levels, phase, total, out, bins):
    cut = own.shape[2]
    pairs = row.shape[1]

    def whole(array):
        return pl.BlockSpec(array.shape, lambda t: (0,) * array.ndim)

    def columns(array):
        return pl.BlockSpec((2, array.shape[1], TILE), lambda t: (0, 0, t))

    blocks = [own, sib, from_own, from_sib]
    ins = [core, row, *blocks, levels, *phase]
    specs = [pl.BlockSpec(memory_space=pltpu.SMEM), whole(row)]
    specs += [columns(b) for b in blocks] + [whole(levels)] + [whole(p) for p in phase]
    scratch = [pltpu.VMEM((bins, pairs), jnp.bfloat16), pltpu.VMEM((2 * TILE, LAGS), jnp.bfloat16)]
    if total is not None:
        ins.append(total)
        specs.append(whole(total))
    is_last = out is not None
    if is_last:
        scratch.append(pltpu.VMEM((bins, LAGS), jnp.float32))
    else:
        out = jax.ShapeDtypeStruct((bins, LAGS), jnp.float32)
    return pl.pallas_call(
        functools.partial(pairs_kernel, first, is_last),
        grid=(cut // TILE,),
        in_specs=specs,
        out_specs=[whole(out)] * (1 + is_last),
        out_shape=[out] * (1 + is_last),
        scratch_shapes=scratch
        + [pltpu.VMEM((pairs // PARTS, 2 * TILE), jnp.bfloat16)] * PARTS,
        compiler_params=params(40),
        cost_estimate=cost(),
        name="add_pairs",
    )(*ins)


def shards(records, chan_pos, bin_row, pair_mask):
    here = lax.axis_index("chan")
    core, chip = here % 2, here // 2
    blocks, bands = lax.axis_size("chan"), lax.axis_size("freq")
    width, _, band = records.shape
    half = width // 2
    bins = bin_row.shape[0]

    core_ref = core.astype(jnp.int32)[None]
    own, own_power, give, give_power = planes(records, core_ref, 0, CUTS[:1])
    sib = [to_sibling(give[0])]
    moved = [to_chips(own[0], (-1, 1)), to_chips(sib[0], (1, -1))]
    records, sib[0] = after(records, sib[0])
    rest_own, more_own, rest, more_give = planes(records, core_ref, CUTS[0], CUTS[1:])
    own, own_power, give_power = own + rest_own, own_power + more_own, give_power + more_give

    totals = lax.psum(jnp.sum(jnp.stack([own_power, give_power]), axis=2), "freq")
    mask = pair_mask[0].astype(jnp.float32)
    own_info = jnp.concatenate([totals[0], mask])
    sib_info = to_sibling(jnp.concatenate([totals[1], mask]))
    own_info_moved = to_chips(own_info, (-1, 1), 1)
    sib_info_moved = to_chips(sib_info, (1, -1), 1)
    phase = phases(lax.axis_index("freq") * band, band // TILE)

    own[1], own_info_moved, phase = after(own[1], own_info_moved, phase)


    sib += [to_sibling(block) for block in rest]
    sib[1], sib_info_moved, moved[1] = after(sib[1], sib_info_moved, moved[1])
    moved += [to_chips(own[1], (-1, 1)), to_chips(sib[1], (1, -1))]

    even_mask = jnp.where(core == 0, mask, sib_info[half:])
    odd_mask = jnp.where(core == 0, sib_info[half:], mask)
    prev_info = jnp.where(core == 0, sib_info_moved, own_info_moved)
    next_info = jnp.where(core == 0, own_info_moved, sib_info_moved)

    totals = jnp.stack([own_info[:half], sib_info[:half], prev_info[:half]], axis=1)
    levels = water * totals / NF + tiny

    places = jnp.pad(chan_pos.reshape(blocks, width), ((1, 1), (0, 0)))
    places = lax.dynamic_slice(places, (2 * chip, core * half), (4, half))
    prev_pos, even_pos, odd_pos, next_pos = places
    apart = jnp.abs(
        jnp.concatenate(
            [odd_pos - even_pos, even_pos - prev_pos, odd_pos - prev_pos, next_pos - even_pos]
        )
    )
    used = jnp.stack(
        [
            odd_mask[0] > 0,
            (even_mask[0] > 0) & (chip > 0),
            (odd_mask[1] > 0) & (chip > 0),
            (next_info[half + 1] > 0) & (chip < blocks // 2 - 1),
        ]
    )
    bin_ids = jnp.arange(bins, dtype=jnp.int32)
    row = jnp.sum(jnp.where(apart[:, None] == bin_ids[None, :], bin_row[None, :], 0), axis=1)
    row = jnp.where(jnp.repeat(used, half), row, -1)
    row = row.reshape(4, PARTS, half // PARTS).transpose(1, 0, 2).reshape(-1)

    out = jax.ShapeDtypeStruct((blocks // 2 * bands, bins // blocks, LAGS // bands), jnp.float32)
    total, start = None, 0
    for k, cut in enumerate(CUTS):
        arrays = own[k], sib[k], moved[2 * k], moved[2 * k + 1]
        goal = out if k == len(CUTS) - 1 else None
        total, *give = add_pairs(
            start // TILE, core_ref, row[None, :], *arrays, levels, phase, total, goal, bins
        )
        if k + 2 < len(CUTS):
            own[k + 2], sib[k + 2], total = after(own[k + 2], sib[k + 2], total)
            moved += [to_chips(own[k + 2], (-1, 1)), to_chips(sib[k + 2], (1, -1))]
        start += cut

    total = (total + to_sibling(*give)).astype(jnp.bfloat16)
    ways = [[i * bands + f for i in range(c, blocks, 2) for f in range(bands)] for c in (0, 1)]
    parts = lax.all_to_all(
        total, ("chan", "freq"), 0, 0, axis_index_groups=ways, tiled=True
    )
    return jnp.sum(parts.astype(jnp.float32), axis=0)


def solution(mesh):
    placed = (P("chan", None, "freq"), P(), P(), P("chan", None))
    return jax.shard_map(
        shards, mesh=mesh, in_specs=placed, out_specs=P("chan", "freq"), check_vma=False
    )
```

```python
import functools
import math

import jax
import jax.numpy as jnp
from jax import lax
from jax.experimental import pallas as pl
from jax.experimental.pallas import tpu as pltpu
from jax.sharding import PartitionSpec as P

NF = 8192
LAGS = 1024

water = 0.5
tiny = 1e-06

TILE = 256
SLAB = 16
FINE = 16
LANES = 128
PARTS = 4
CUTS = (1024, 768, 256)


def params(mebibytes=57):
    return pltpu.CompilerParams(vmem_limit_bytes=mebibytes * 1024 * 1024)


def cost():
    return pl.CostEstimate(flops=1, bytes_accessed=1, transcendentals=0)


def after(*arrays):
    return lax.optimization_barrier(arrays)


def to_sibling(block):
    return lax.ppermute(block, "chan", [(i, i ^ 1) for i in range(lax.axis_size("chan"))])


def to_chips(block, core_steps, bands=0):
    devices, count = range(lax.axis_size("chan")), lax.axis_size("freq")
    route = [(i, i + 2 * core_steps[i % 2]) for i in devices]
    route = [(i, j) for i, j in route if j in devices]
    if not bands:
        return lax.ppermute(block, "chan", route)
    route = [
        (i * count + f, j * count + (f + bands) % count) for i, j in route for f in range(count)
    ]
    return lax.ppermute(block, ("chan", "freq"), route)


def phases(first, tiles):
    tile = first + TILE * jnp.arange(tiles, dtype=jnp.int32)
    coarse = FINE * jnp.arange(TILE // FINE, dtype=jnp.int32)
    freqs = jnp.concatenate([tile, coarse, jnp.arange(FINE, dtype=jnp.int32)])
    lagvec = jnp.arange(LAGS, dtype=jnp.int32) - LAGS // 2
    phase = jnp.mod(freqs[:, None] * lagvec[None, :], 2 * NF)
    theta = 2.0 * math.pi / (2 * NF) * phase.astype(jnp.float32)
    scale = jnp.where(jnp.arange(len(freqs)) < tiles, 1.0 / math.sqrt(NF), 1.0)[:, None]
    return jnp.cos(theta) * scale, -jnp.sin(theta) * scale


def turned(one, other):
    return one[0] * other[0] - one[1] * other[1], one[1] * other[0] + one[0] * other[1]


def planes_kernel(column, core_ref, *refs):
    count = (len(refs) - 4) // 2
    for n, records_ref in enumerate(refs[:2]):
        *planes_refs, power_ref = refs[2 + n * (count + 1) : 2 + (n + 1) * (count + 1)]
        channels, _, width = records_ref.shape
        width -= column
        for s in range(0, channels, SLAB):
            planes = jnp.swapaxes(records_ref[s : s + SLAB, :, column:], 0, 1)
            start = 0
            for ref in planes_refs:
                cut = ref.shape[2]
                ref[:, s : s + SLAB, :] = planes[:, :, start : start + cut]
                start += cut
            re, im = planes[0].astype(jnp.float32), planes[1].astype(jnp.float32)
            power = re * re + im * im
            total = power[:, :LANES]
            for f in range(LANES, width, LANES):
                total += power[:, f : f + LANES]
            power_ref[s : s + SLAB, :] = total


def planes(records, core, start, cuts):
    half = records.shape[0] // 2
    width = sum(cuts)
    aligned = start % width == 0
    loaded, column = (width, start // width) if aligned else (records.shape[2], 0)
    block = 256
    steps = half // block
    outs = [pl.BlockSpec((2, block, cut), lambda t, c: (0, t, 0)) for cut in cuts]
    outs += [pl.BlockSpec((block, LANES), lambda t, c: (t, 0))]
    shapes = [jax.ShapeDtypeStruct((2, half, cut), jnp.bfloat16) for cut in cuts]
    shapes += [jax.ShapeDtypeStruct((half, LANES), jnp.float32)]
    spec = pltpu.PrefetchScalarGridSpec(
        num_scalar_prefetch=1,
        grid=(steps,),
        in_specs=[
            pl.BlockSpec((block, 2, loaded), lambda t, c: (c[0] * steps + t, 0, column)),
            pl.BlockSpec((block, 2, loaded), lambda t, c: ((1 - c[0]) * steps + t, 0, column)),
        ],
        out_specs=outs * 2,
    )
    results = pl.pallas_call(
        functools.partial(planes_kernel, 0 if aligned else start),
        grid_spec=spec,
        out_shape=shapes * 2,
        compiler_params=params(),
        cost_estimate=cost(),
        name="planes",
    )(core, records, records)
    n = len(cuts)
    return list(results[:n]), results[n], list(results[n + 1 : -1]), results[-1]


def load(ref, rows):
    return ref[0, rows, :].astype(jnp.float32), ref[1, rows, :].astype(jnp.float32)


def whiten(spectrum, level):
    re, im = spectrum
    inverse = pltpu.reciprocal(re * re + im * im + level, approx=True)
    return (
        (re * inverse).astype(jnp.bfloat16).astype(jnp.float32),
        (im * inverse).astype(jnp.bfloat16).astype(jnp.float32),
    )


def pairs_kernel(first, is_last, core, row_ref, own, sib, from_own, from_sib, *refs):
    levels, cos_ref, sin_ref, *refs = refs
    total_in = refs.pop(0) if first else None
    out_ref, *refs = refs
    give_ref = refs.pop(0) if is_last else None
    onehot, table, *refs = refs
    total = refs.pop(0) if is_last else out_ref
    step = pl.program_id(0)
    count = own.shape[1] // len(refs)

    @pl.when(step == 0)
    def _():
        bins, pairs = onehot.shape
        for k in range(0, pairs, 256):
            bin_row = lax.broadcasted_iota(jnp.int32, (bins, 256), 0)
            hit = bin_row == row_ref[:, k : k + 256]
            onehot[:, k : k + 256] = jnp.where(hit, 1.0, 0.0).astype(jnp.bfloat16)

    def fill_table():
        tiles = cos_ref.shape[0] - TILE // FINE - FINE
        start = pl.ds(first + step, 1)
        coarse, fine = slice(tiles, tiles + TILE // FINE), slice(tiles + TILE // FINE, None)
        turn = turned(
            (cos_ref[start, :], sin_ref[start, :]), (cos_ref[coarse, :], sin_ref[coarse, :])
        )
        steps = cos_ref[fine, :], sin_ref[fine, :]
        for a in range(TILE // FINE):
            rows = slice(a * FINE, (a + 1) * FINE)
            cos, sin = turned([part[a : a + 1, :] for part in turn], steps)
            table[rows, :] = cos.astype(jnp.bfloat16)
            table[TILE + a * FINE : TILE + (a + 1) * FINE, :] = sin.astype(jnp.bfloat16)

    def products(prods, start, even, odd, even_level, prev, after):
        for s in range(0, count, SLAB):
            rows = slice(start + s, start + s + SLAB)

            def put(slot, receiver, source):
                rre, rim = receiver
                wre, wim = source
                to = slice(slot * count + s, slot * count + s + SLAB)
                prods[to, :TILE] = (rre * wre + rim * wim).astype(jnp.bfloat16)
                prods[to, TILE:] = (rim * wre - rre * wim).astype(jnp.bfloat16)

            even_rec, odd_rec = load(even, rows), load(odd, rows)
            even_white = whiten(even_rec, levels[rows, even_level : even_level + 1])
            prev_white = whiten(load(prev, rows), levels[rows, 2:3])
            put(0, odd_rec, even_white)
            put(1, even_rec, prev_white)
            put(2, odd_rec, prev_white)
            put(3, load(after, rows), even_white)

    def run(*blocks):
        fill_table()
        stack = None
        for part, prods in enumerate(refs):
            products(prods, part * count, *blocks)
            pairs = slice(part * 4 * count, (part + 1) * 4 * count)
            sums = jnp.dot(onehot[:, pairs], prods[...], preferred_element_type=jnp.float32)
            stack = sums if stack is None else stack + sums
        stack = stack.astype(jnp.bfloat16)
        lagged = jnp.dot(stack, table[...], preferred_element_type=jnp.float32)

        @pl.when(step == 0)
        def _():
            total[...] = total_in[...] + lagged if first else lagged

        @pl.when(step > 0)
        def _():
            total[...] += lagged

    pl.when(core[0] == 0)(lambda: run(own, sib, 0, from_sib, from_own))
    pl.when(core[0] != 0)(lambda: run(sib, own, 1, from_own, from_sib))

    if is_last:
        parts, rows, lags = out_ref.shape
        bands = total.shape[1] // lags

        @pl.when(step == pl.num_programs(0) - 1)
        def _():
            for part in range(parts):
                chip, f = part // bands, part % bands * lags
                for ref, owner in ((out_ref, core[0]), (give_ref, 1 - core[0])):
                    start = pl.multiple_of((2 * chip + owner) * rows, rows)
                    ref[part] = total[pl.ds(start, rows), f : f + lags]


def add_pairs(first, core, row, own, sib, from_own, from_sib, levels, phase, total, out, bins):
    cut = own.shape[2]
    pairs = row.shape[1]

    def whole(array):
        return pl.BlockSpec(array.shape, lambda t: (0,) * array.ndim)

    def columns(array):
        return pl.BlockSpec((2, array.shape[1], TILE), lambda t: (0, 0, t))

    blocks = [own, sib, from_own, from_sib]
    ins = [core, row, *blocks, levels, *phase]
    specs = [pl.BlockSpec(memory_space=pltpu.SMEM), whole(row)]
    specs += [columns(b) for b in blocks] + [whole(levels)] + [whole(p) for p in phase]
    scratch = [pltpu.VMEM((bins, pairs), jnp.bfloat16), pltpu.VMEM((2 * TILE, LAGS), jnp.bfloat16)]
    if total is not None:
        ins.append(total)
        specs.append(whole(total))
    is_last = out is not None
    if is_last:
        scratch.append(pltpu.VMEM((bins, LAGS), jnp.float32))
    else:
        out = jax.ShapeDtypeStruct((bins, LAGS), jnp.float32)
    return pl.pallas_call(
        functools.partial(pairs_kernel, first, is_last),
        grid=(cut // TILE,),
        in_specs=specs,
        out_specs=[whole(out)] * (1 + is_last),
        out_shape=[out] * (1 + is_last),
        scratch_shapes=scratch
        + [pltpu.VMEM((pairs // PARTS, 2 * TILE), jnp.bfloat16)] * PARTS,
        compiler_params=params(40),
        cost_estimate=cost(),
        name="add_pairs",
    )(*ins)


def shards(records, chan_pos, bin_row, pair_mask):
    here = lax.axis_index("chan")
    core, chip = here % 2, here // 2
    blocks, bands = lax.axis_size("chan"), lax.axis_size("freq")
    width, _, band = records.shape
    half = width // 2
    bins = bin_row.shape[0]

    core_ref = core.astype(jnp.int32)[None]
    own, own_power, give, give_power = planes(records, core_ref, 0, CUTS[:1])
    sib = [to_sibling(give[0])]
    moved = [to_chips(own[0], (-1, 1)), to_chips(sib[0], (1, -1))]
    records, sib[0] = after(records, sib[0])
    rest_own, more_own, rest, more_give = planes(records, core_ref, CUTS[0], CUTS[1:])
    own, own_power, give_power = own + rest_own, own_power + more_own, give_power + more_give

    totals = lax.psum(jnp.sum(jnp.stack([own_power, give_power]), axis=2), "freq")
    mask = pair_mask[0].astype(jnp.float32)
    own_info = jnp.concatenate([totals[0], mask])
    sib_info = to_sibling(jnp.concatenate([totals[1], mask]))
    own_info_moved = to_chips(own_info, (-1, 1), 1)
    sib_info_moved = to_chips(sib_info, (1, -1), 1)
    phase = phases(lax.axis_index("freq") * band, band // TILE)

    own[1], own_info_moved, phase = after(own[1], own_info_moved, phase)


    sib += [to_sibling(block) for block in rest]
    sib[1], sib_info_moved, moved[1] = after(sib[1], sib_info_moved, moved[1])
    moved += [to_chips(own[1], (-1, 1)), to_chips(sib[1], (1, -1))]

    even_mask = jnp.where(core == 0, mask, sib_info[half:])
    odd_mask = jnp.where(core == 0, sib_info[half:], mask)
    prev_info = jnp.where(core == 0, sib_info_moved, own_info_moved)
    next_info = jnp.where(core == 0, own_info_moved, sib_info_moved)

    totals = jnp.stack([own_info[:half], sib_info[:half], prev_info[:half]], axis=1)
    levels = water * totals / NF + tiny

    places = jnp.pad(chan_pos.reshape(blocks, width), ((1, 1), (0, 0)))
    places = lax.dynamic_slice(places, (2 * chip, core * half), (4, half))
    prev_pos, even_pos, odd_pos, next_pos = places
    apart = jnp.abs(
        jnp.concatenate(
            [odd_pos - even_pos, even_pos - prev_pos, odd_pos - prev_pos, next_pos - even_pos]
        )
    )
    used = jnp.stack(
        [
            odd_mask[0] > 0,
            (even_mask[0] > 0) & (chip > 0),
            (odd_mask[1] > 0) & (chip > 0),
            (next_info[half + 1] > 0) & (chip < blocks // 2 - 1),
        ]
    )
    bin_ids = jnp.arange(bins, dtype=jnp.int32)
    row = jnp.sum(jnp.where(apart[:, None] == bin_ids[None, :], bin_row[None, :], 0), axis=1)
    row = jnp.where(jnp.repeat(used, half), row, -1)
    row = row.reshape(4, PARTS, half // PARTS).transpose(1, 0, 2).reshape(-1)

    out = jax.ShapeDtypeStruct((blocks // 2 * bands, bins // blocks, LAGS // bands), jnp.float32)
    total, start = None, 0
    for k, cut in enumerate(CUTS):
        arrays = own[k], sib[k], moved[2 * k], moved[2 * k + 1]
        goal = out if k == len(CUTS) - 1 else None
        total, *give = add_pairs(
            start // TILE, core_ref, row[None, :], *arrays, levels, phase, total, goal, bins
        )
        if k + 2 < len(CUTS):
            own[k + 2], sib[k + 2], total = after(own[k + 2], sib[k + 2], total)
            moved += [to_chips(own[k + 2], (-1, 1)), to_chips(sib[k + 2], (1, -1))]
        start += cut

    total = (total + to_sibling(*give)).astype(jnp.bfloat16)
    ways = [[i * bands + f for i in range(c, blocks, 2) for f in range(bands)] for c in (0, 1)]
    parts = lax.all_to_all(
        total, ("chan", "freq"), 0, 0, axis_index_groups=ways, tiled=True
    )
    return jnp.sum(parts.astype(jnp.float32), axis=0)


def solution(mesh):
    placed = (P("chan", None, "freq"), P(), P(), P("chan", None))
    return jax.shard_map(
        shards, mesh=mesh, in_specs=placed, out_specs=P("chan", "freq"), check_vma=False
    )
```

```python
import functools
import math

import jax
import jax.numpy as jnp
from jax import lax
from jax.experimental import pallas as pl
from jax.experimental.pallas import tpu as pltpu
from jax.sharding import PartitionSpec as P

NF = 8192
LAGS = 1024

water = 0.5
tiny = 1e-06

TILE = 256
SLAB = 16
FINE = 16
LANES = 128
PARTS = 4
CUTS = (1024, 768, 256)


def params(mebibytes=57):
    return pltpu.CompilerParams(vmem_limit_bytes=mebibytes * 1024 * 1024)


def cost():
    return pl.CostEstimate(flops=1, bytes_accessed=1, transcendentals=0)


def after(*arrays):
    return lax.optimization_barrier(arrays)


def to_sibling(block):
    return lax.ppermute(block, "chan", [(i, i ^ 1) for i in range(lax.axis_size("chan"))])


def to_chips(block, core_steps, bands=0):
    devices, count = range(lax.axis_size("chan")), lax.axis_size("freq")
    route = [(i, i + 2 * core_steps[i % 2]) for i in devices]
    route = [(i, j) for i, j in route if j in devices]
    if not bands:
        return lax.ppermute(block, "chan", route)
    route = [
        (i * count + f, j * count + (f + bands) % count) for i, j in route for f in range(count)
    ]
    return lax.ppermute(block, ("chan", "freq"), route)


def phases(first, tiles):
    tile = first + TILE * jnp.arange(tiles, dtype=jnp.int32)
    coarse = FINE * jnp.arange(TILE // FINE, dtype=jnp.int32)
    freqs = jnp.concatenate([tile, coarse, jnp.arange(FINE, dtype=jnp.int32)])
    lagvec = jnp.arange(LAGS, dtype=jnp.int32) - LAGS // 2
    phase = jnp.mod(freqs[:, None] * lagvec[None, :], 2 * NF)
    theta = 2.0 * math.pi / (2 * NF) * phase.astype(jnp.float32)
    scale = jnp.where(jnp.arange(len(freqs)) < tiles, 1.0 / math.sqrt(NF), 1.0)[:, None]
    return jnp.cos(theta) * scale, -jnp.sin(theta) * scale


def turned(one, other):
    return one[0] * other[0] - one[1] * other[1], one[1] * other[0] + one[0] * other[1]


def power_of(planes):
    re, im = planes[0].astype(jnp.float32), planes[1].astype(jnp.float32)
    power = re * re + im * im
    total = power[:, :LANES]
    for f in range(LANES, power.shape[1], LANES):
        total += power[:, f : f + LANES]
    return total


def planes_kernel(with_power, core_ref, *refs):
    count = len(refs) // 2 - 1
    for n, records_ref in enumerate(refs[:2]):
        outs = refs[2 + n * count : 2 + (n + 1) * count]
        for s in range(0, records_ref.shape[0], SLAB):
            planes = jnp.swapaxes(records_ref[s : s + SLAB], 0, 1)
            start = 0
            for ref in outs[: count - with_power]:
                cut = ref.shape[2]
                ref[:, s : s + SLAB, :] = planes[:, :, start : start + cut]
                start += cut
            if with_power:
                outs[-1][s : s + SLAB, :] = power_of(planes)


def planes(records, core, start, cuts, with_power):
    half = records.shape[0] // 2
    width = sum(cuts)
    column = start // width
    block = 256
    steps = half // block
    outs = [pl.BlockSpec((2, block, cut), lambda t, c: (0, t, 0)) for cut in cuts]
    shapes = [jax.ShapeDtypeStruct((2, half, cut), jnp.bfloat16) for cut in cuts]
    if with_power:
        outs += [pl.BlockSpec((block, LANES), lambda t, c: (t, 0))]
        shapes += [jax.ShapeDtypeStruct((half, LANES), jnp.float32)]
    spec = pltpu.PrefetchScalarGridSpec(
        num_scalar_prefetch=1,
        grid=(steps,),
        in_specs=[
            pl.BlockSpec((block, 2, width), lambda t, c: (c[0] * steps + t, 0, column)),
            pl.BlockSpec((block, 2, width), lambda t, c: ((1 - c[0]) * steps + t, 0, column)),
        ],
        out_specs=outs * 2,
    )
    results = pl.pallas_call(
        functools.partial(planes_kernel, int(with_power)),
        grid_spec=spec,
        out_shape=shapes * 2,
        compiler_params=params(),
        cost_estimate=cost(),
        name="planes",
    )(core, records, records)
    return list(results[: len(outs)]), list(results[len(outs) :])


def power_kernel(*refs):
    for planes_ref, power_ref in zip(refs[:2], refs[2:]):
        for s in range(0, planes_ref.shape[1], SLAB):
            power_ref[s : s + SLAB, :] = power_of(planes_ref[:, s : s + SLAB, :])


def powers(*blocks):
    _, channels, width = blocks[0].shape
    block = channels // 2
    out = jax.ShapeDtypeStruct((channels, LANES), jnp.float32)
    return pl.pallas_call(
        power_kernel,
        grid=(channels // block,),
        in_specs=[pl.BlockSpec((2, block, width), lambda t: (0, t, 0))] * 2,
        out_specs=[pl.BlockSpec((block, LANES), lambda t: (t, 0))] * 2,
        out_shape=[out, out],
        compiler_params=params(),
        cost_estimate=cost(),
        name="powers",
    )(*blocks)


def load(ref, rows):
    return ref[0, rows, :].astype(jnp.float32), ref[1, rows, :].astype(jnp.float32)


def whiten(spectrum, level):
    re, im = spectrum
    inverse = pltpu.reciprocal(re * re + im * im + level, approx=True)
    return (
        (re * inverse).astype(jnp.bfloat16).astype(jnp.float32),
        (im * inverse).astype(jnp.bfloat16).astype(jnp.float32),
    )


def pairs_kernel(first, is_last, core, row_ref, own, sib, from_own, from_sib, *refs):
    levels, cos_ref, sin_ref, *refs = refs
    total_in = refs.pop(0) if first else None
    out_ref, *refs = refs
    give_ref = refs.pop(0) if is_last else None
    onehot, table, *refs = refs
    total = refs.pop(0) if is_last else out_ref
    step = pl.program_id(0)
    count = own.shape[1] // len(refs)

    @pl.when(step == 0)
    def _():
        bins, pairs = onehot.shape
        for k in range(0, pairs, 256):
            bin_row = lax.broadcasted_iota(jnp.int32, (bins, 256), 0)
            hit = bin_row == row_ref[:, k : k + 256]
            onehot[:, k : k + 256] = jnp.where(hit, 1.0, 0.0).astype(jnp.bfloat16)

    def fill_table():
        tiles = cos_ref.shape[0] - TILE // FINE - FINE
        start = pl.ds(first + step, 1)
        coarse, fine = slice(tiles, tiles + TILE // FINE), slice(tiles + TILE // FINE, None)
        turn = turned(
            (cos_ref[start, :], sin_ref[start, :]), (cos_ref[coarse, :], sin_ref[coarse, :])
        )
        steps = cos_ref[fine, :], sin_ref[fine, :]
        for a in range(TILE // FINE):
            rows = slice(a * FINE, (a + 1) * FINE)
            cos, sin = turned([part[a : a + 1, :] for part in turn], steps)
            table[rows, :] = cos.astype(jnp.bfloat16)
            table[TILE + a * FINE : TILE + (a + 1) * FINE, :] = sin.astype(jnp.bfloat16)

    def products(prods, start, even, odd, even_level, prev, after):
        for s in range(0, count, SLAB):
            rows = slice(start + s, start + s + SLAB)

            def put(slot, receiver, source):
                rre, rim = receiver
                wre, wim = source
                to = slice(slot * count + s, slot * count + s + SLAB)
                prods[to, :TILE] = (rre * wre + rim * wim).astype(jnp.bfloat16)
                prods[to, TILE:] = (rim * wre - rre * wim).astype(jnp.bfloat16)

            even_rec, odd_rec = load(even, rows), load(odd, rows)
            even_white = whiten(even_rec, levels[rows, even_level : even_level + 1])
            prev_white = whiten(load(prev, rows), levels[rows, 2:3])
            put(0, odd_rec, even_white)
            put(1, even_rec, prev_white)
            put(2, odd_rec, prev_white)
            put(3, load(after, rows), even_white)

    def run(*blocks):
        fill_table()
        stack = None
        for part, prods in enumerate(refs):
            products(prods, part * count, *blocks)
            pairs = slice(part * 4 * count, (part + 1) * 4 * count)
            sums = jnp.dot(onehot[:, pairs], prods[...], preferred_element_type=jnp.float32)
            stack = sums if stack is None else stack + sums
        stack = stack.astype(jnp.bfloat16)
        lagged = jnp.dot(stack, table[...], preferred_element_type=jnp.float32)

        @pl.when(step == 0)
        def _():
            total[...] = total_in[...] + lagged if first else lagged

        @pl.when(step > 0)
        def _():
            total[...] += lagged

    pl.when(core[0] == 0)(lambda: run(own, sib, 0, from_sib, from_own))
    pl.when(core[0] != 0)(lambda: run(sib, own, 1, from_own, from_sib))

    if is_last:
        parts, rows, lags = out_ref.shape
        bands = total.shape[1] // lags

        @pl.when(step == pl.num_programs(0) - 1)
        def _():
            for part in range(parts):
                chip, f = part // bands, part % bands * lags
                for ref, owner in ((out_ref, core[0]), (give_ref, 1 - core[0])):
                    start = pl.multiple_of((2 * chip + owner) * rows, rows)
                    ref[part] = total[pl.ds(start, rows), f : f + lags]


def add_pairs(first, core, row, own, sib, from_own, from_sib, levels, phase, total, out, bins):
    cut = own.shape[2]
    pairs = row.shape[1]

    def whole(array):
        return pl.BlockSpec(array.shape, lambda t: (0,) * array.ndim)

    def columns(array):
        return pl.BlockSpec((2, array.shape[1], TILE), lambda t: (0, 0, t))

    blocks = [own, sib, from_own, from_sib]
    ins = [core, row, *blocks, levels, *phase]
    specs = [pl.BlockSpec(memory_space=pltpu.SMEM), whole(row)]
    specs += [columns(b) for b in blocks] + [whole(levels)] + [whole(p) for p in phase]
    scratch = [pltpu.VMEM((bins, pairs), jnp.bfloat16), pltpu.VMEM((2 * TILE, LAGS), jnp.bfloat16)]
    if total is not None:
        ins.append(total)
        specs.append(whole(total))
    is_last = out is not None
    if is_last:
        scratch.append(pltpu.VMEM((bins, LAGS), jnp.float32))
    else:
        out = jax.ShapeDtypeStruct((bins, LAGS), jnp.float32)
    return pl.pallas_call(
        functools.partial(pairs_kernel, first, is_last),
        grid=(cut // TILE,),
        in_specs=specs,
        out_specs=[whole(out)] * (1 + is_last),
        out_shape=[out] * (1 + is_last),
        scratch_shapes=scratch
        + [pltpu.VMEM((pairs // PARTS, 2 * TILE), jnp.bfloat16)] * PARTS,
        compiler_params=params(40),
        cost_estimate=cost(),
        name="add_pairs",
    )(*ins)


def shards(records, chan_pos, bin_row, pair_mask):
    here = lax.axis_index("chan")
    core, chip = here % 2, here // 2
    blocks, bands = lax.axis_size("chan"), lax.axis_size("freq")
    width, _, band = records.shape
    half = width // 2
    bins = bin_row.shape[0]

    core_ref = core.astype(jnp.int32)[None]
    own, give = planes(records, core_ref, 0, CUTS[:1], False)
    own_power, give_power = powers(own[0], give[0])
    sib = [to_sibling(give[0])]
    moved = [to_chips(own[0], (-1, 1)), to_chips(sib[0], (1, -1))]
    records, sib[0] = after(records, sib[0])
    (*rest_own, more_own), (*rest, more_give) = planes(
        records, core_ref, CUTS[0], CUTS[1:], True
    )
    own, own_power, give_power = own + rest_own, own_power + more_own, give_power + more_give

    totals = lax.psum(jnp.sum(jnp.stack([own_power, give_power]), axis=2), "freq")
    mask = pair_mask[0].astype(jnp.float32)
    own_info = jnp.concatenate([totals[0], mask])
    sib_info = to_sibling(jnp.concatenate([totals[1], mask]))
    own_info_moved = to_chips(own_info, (-1, 1), 1)
    sib_info_moved = to_chips(sib_info, (1, -1), 1)
    phase = phases(lax.axis_index("freq") * band, band // TILE)

    own[1], own_info_moved, phase = after(own[1], own_info_moved, phase)


    sib += [to_sibling(block) for block in rest]
    sib[1], sib_info_moved, moved[1] = after(sib[1], sib_info_moved, moved[1])
    moved += [to_chips(own[1], (-1, 1)), to_chips(sib[1], (1, -1))]

    even_mask = jnp.where(core == 0, mask, sib_info[half:])
    odd_mask = jnp.where(core == 0, sib_info[half:], mask)
    prev_info = jnp.where(core == 0, sib_info_moved, own_info_moved)
    next_info = jnp.where(core == 0, own_info_moved, sib_info_moved)

    totals = jnp.stack([own_info[:half], sib_info[:half], prev_info[:half]], axis=1)
    levels = water * totals / NF + tiny

    places = jnp.pad(chan_pos.reshape(blocks, width), ((1, 1), (0, 0)))
    places = lax.dynamic_slice(places, (2 * chip, core * half), (4, half))
    prev_pos, even_pos, odd_pos, next_pos = places
    apart = jnp.abs(
        jnp.concatenate(
            [odd_pos - even_pos, even_pos - prev_pos, odd_pos - prev_pos, next_pos - even_pos]
        )
    )
    used = jnp.stack(
        [
            odd_mask[0] > 0,
            (even_mask[0] > 0) & (chip > 0),
            (odd_mask[1] > 0) & (chip > 0),
            (next_info[half + 1] > 0) & (chip < blocks // 2 - 1),
        ]
    )
    bin_ids = jnp.arange(bins, dtype=jnp.int32)
    row = jnp.sum(jnp.where(apart[:, None] == bin_ids[None, :], bin_row[None, :], 0), axis=1)
    row = jnp.where(jnp.repeat(used, half), row, -1)
    row = row.reshape(4, PARTS, half // PARTS).transpose(1, 0, 2).reshape(-1)

    out = jax.ShapeDtypeStruct((blocks // 2 * bands, bins // blocks, LAGS // bands), jnp.float32)
    total, start = None, 0
    for k, cut in enumerate(CUTS):
        arrays = own[k], sib[k], moved[2 * k], moved[2 * k + 1]
        goal = out if k == len(CUTS) - 1 else None
        total, *give = add_pairs(
            start // TILE, core_ref, row[None, :], *arrays, levels, phase, total, goal, bins
        )
        if k + 2 < len(CUTS):
            own[k + 2], sib[k + 2], total = after(own[k + 2], sib[k + 2], total)
            moved += [to_chips(own[k + 2], (-1, 1)), to_chips(sib[k + 2], (1, -1))]
        start += cut

    total = (total + to_sibling(*give)).astype(jnp.bfloat16)
    ways = [[i * bands + f for i in range(c, blocks, 2) for f in range(bands)] for c in (0, 1)]
    parts = lax.all_to_all(
        total, ("chan", "freq"), 0, 0, axis_index_groups=ways, tiled=True
    )
    return jnp.sum(parts.astype(jnp.float32), axis=0)


def solution(mesh):
    placed = (P("chan", None, "freq"), P(), P(), P("chan", None))
    return jax.shard_map(
        shards, mesh=mesh, in_specs=placed, out_specs=P("chan", "freq"), check_vma=False
    )
```

```python
import functools
import math

import jax
import jax.numpy as jnp
from jax import lax
from jax.experimental import pallas as pl
from jax.experimental.pallas import tpu as pltpu
from jax.sharding import PartitionSpec as P

NF = 8192
LAGS = 1024

water = 0.5
tiny = 1e-06

TILE = 256
SLAB = 16
FINE = 16
LANES = 128
PARTS = 4
CUTS = (1024, 768, 256)


def params(mebibytes=57):
    return pltpu.CompilerParams(vmem_limit_bytes=mebibytes * 1024 * 1024)


def cost():
    return pl.CostEstimate(flops=1, bytes_accessed=1, transcendentals=0)


def after(*arrays):
    return lax.optimization_barrier(arrays)


def to_sibling(block):
    return lax.ppermute(block, "chan", [(i, i ^ 1) for i in range(lax.axis_size("chan"))])


def to_chips(block, core_steps, bands=0):
    devices, count = range(lax.axis_size("chan")), lax.axis_size("freq")
    route = [(i, i + 2 * core_steps[i % 2]) for i in devices]
    route = [(i, j) for i, j in route if j in devices]
    if not bands:
        return lax.ppermute(block, "chan", route)
    route = [
        (i * count + f, j * count + (f + bands) % count) for i, j in route for f in range(count)
    ]
    return lax.ppermute(block, ("chan", "freq"), route)


def phases(first, tiles):
    tile = first + TILE * jnp.arange(tiles, dtype=jnp.int32)
    coarse = FINE * jnp.arange(TILE // FINE, dtype=jnp.int32)
    freqs = jnp.concatenate([tile, coarse, jnp.arange(FINE, dtype=jnp.int32)])
    lagvec = jnp.arange(LAGS, dtype=jnp.int32) - LAGS // 2
    phase = jnp.mod(freqs[:, None] * lagvec[None, :], 2 * NF)
    theta = 2.0 * math.pi / (2 * NF) * phase.astype(jnp.float32)
    scale = jnp.where(jnp.arange(len(freqs)) < tiles, 1.0 / math.sqrt(NF), 1.0)[:, None]
    return jnp.cos(theta) * scale, -jnp.sin(theta) * scale


def turned(one, other):
    return one[0] * other[0] - one[1] * other[1], one[1] * other[0] + one[0] * other[1]


def power_of(planes):
    re, im = planes[0].astype(jnp.float32), planes[1].astype(jnp.float32)
    power = re * re + im * im
    total = power[:, :LANES]
    for f in range(LANES, power.shape[1], LANES):
        total += power[:, f : f + LANES]
    return total


def planes_kernel(with_power, core_ref, *refs):
    count = len(refs) // 2 - 1
    for n, records_ref in enumerate(refs[:2]):
        outs = refs[2 + n * count : 2 + (n + 1) * count]
        for s in range(0, records_ref.shape[0], SLAB):
            planes = jnp.swapaxes(records_ref[s : s + SLAB], 0, 1)
            start = 0
            for ref in outs[: count - with_power]:
                cut = ref.shape[2]
                ref[:, s : s + SLAB, :] = planes[:, :, start : start + cut]
                start += cut
            if with_power:
                outs[-1][s : s + SLAB, :] = power_of(planes)


def planes(records, core, start, cuts, with_power):
    half = records.shape[0] // 2
    width = sum(cuts)
    column = start // width
    block = 256
    steps = half // block
    outs = [pl.BlockSpec((2, block, cut), lambda t, c: (0, t, 0)) for cut in cuts]
    shapes = [jax.ShapeDtypeStruct((2, half, cut), jnp.bfloat16) for cut in cuts]
    if with_power:
        outs += [pl.BlockSpec((block, LANES), lambda t, c: (t, 0))]
        shapes += [jax.ShapeDtypeStruct((half, LANES), jnp.float32)]
    spec = pltpu.PrefetchScalarGridSpec(
        num_scalar_prefetch=1,
        grid=(steps,),
        in_specs=[
            pl.BlockSpec((block, 2, width), lambda t, c: (c[0] * steps + t, 0, column)),
            pl.BlockSpec((block, 2, width), lambda t, c: ((1 - c[0]) * steps + t, 0, column)),
        ],
        out_specs=outs * 2,
    )
    results = pl.pallas_call(
        functools.partial(planes_kernel, int(with_power)),
        grid_spec=spec,
        out_shape=shapes * 2,
        compiler_params=params(),
        cost_estimate=cost(),
        name="planes",
    )(core, records, records)
    return list(results[: len(outs)]), list(results[len(outs) :])


def head_kernel(core_ref, records_ref, own_ref, give_ref, raw, done, came, gone):
    _, half, width = own_ref.shape
    pieces, block = raw.shape[:2]
    per_side = pieces // 2

    def copy_in(n):
        side, row = n // per_side, n % per_side * block
        first = (core_ref[0] if side == 0 else 1 - core_ref[0]) * half + row
        rows = pl.ds(pl.multiple_of(first, block), block)
        return pltpu.make_async_copy(records_ref.at[rows, :, :width], raw.at[n], came.at[n])

    def copy_out(n):
        out_ref, row = (own_ref, give_ref)[n // per_side], n % per_side * block
        return pltpu.make_async_copy(done.at[n], out_ref.at[:, row : row + block, :], gone.at[n])

    for n in range(pieces):
        copy_in(n).start()
    for n in range(pieces):
        copy_in(n).wait()
        for s in range(0, block, SLAB):
            done[n, :, s : s + SLAB, :] = jnp.swapaxes(raw[n, s : s + SLAB], 0, 1)
        copy_out(n).start()
    for n in range(pieces):
        copy_out(n).wait()


def head_planes(records, core, width):
    half = records.shape[0] // 2
    pieces, block = 8, half // 4
    out = jax.ShapeDtypeStruct((2, half, width), jnp.bfloat16)
    return pl.pallas_call(
        head_kernel,
        in_specs=[pl.BlockSpec(memory_space=pltpu.SMEM), pl.BlockSpec(memory_space=pl.ANY)],
        out_specs=[pl.BlockSpec(memory_space=pl.ANY)] * 2,
        out_shape=[out, out],
        scratch_shapes=[
            pltpu.VMEM((pieces, block, 2, width), jnp.bfloat16),
            pltpu.VMEM((pieces, 2, block, width), jnp.bfloat16),
            pltpu.SemaphoreType.DMA((pieces,)),
            pltpu.SemaphoreType.DMA((pieces,)),
        ],
        compiler_params=params(),
        cost_estimate=cost(),
        name="head_planes",
    )(core, records)


def power_kernel(*refs):
    for planes_ref, power_ref in zip(refs[:2], refs[2:]):
        for s in range(0, planes_ref.shape[1], SLAB):
            power_ref[s : s + SLAB, :] = power_of(planes_ref[:, s : s + SLAB, :])


def powers(*blocks):
    _, channels, width = blocks[0].shape
    block = channels // 2
    out = jax.ShapeDtypeStruct((channels, LANES), jnp.float32)
    return pl.pallas_call(
        power_kernel,
        grid=(channels // block,),
        in_specs=[pl.BlockSpec((2, block, width), lambda t: (0, t, 0))] * 2,
        out_specs=[pl.BlockSpec((block, LANES), lambda t: (t, 0))] * 2,
        out_shape=[out, out],
        compiler_params=params(),
        cost_estimate=cost(),
        name="powers",
    )(*blocks)


def load(ref, rows):
    return ref[0, rows, :].astype(jnp.float32), ref[1, rows, :].astype(jnp.float32)


def whiten(spectrum, level):
    re, im = spectrum
    inverse = pltpu.reciprocal(re * re + im * im + level, approx=True)
    return (
        (re * inverse).astype(jnp.bfloat16).astype(jnp.float32),
        (im * inverse).astype(jnp.bfloat16).astype(jnp.float32),
    )


def pairs_kernel(first, is_last, core, row_ref, own, sib, from_own, from_sib, *refs):
    levels, cos_ref, sin_ref, *refs = refs
    total_in = refs.pop(0) if first else None
    out_ref, *refs = refs
    give_ref = refs.pop(0) if is_last else None
    onehot, table, *refs = refs
    total = refs.pop(0) if is_last else out_ref
    step = pl.program_id(0)
    count = own.shape[1] // len(refs)

    @pl.when(step == 0)
    def _():
        bins, pairs = onehot.shape
        for k in range(0, pairs, 256):
            bin_row = lax.broadcasted_iota(jnp.int32, (bins, 256), 0)
            hit = bin_row == row_ref[:, k : k + 256]
            onehot[:, k : k + 256] = jnp.where(hit, 1.0, 0.0).astype(jnp.bfloat16)

    def fill_table():
        tiles = cos_ref.shape[0] - TILE // FINE - FINE
        start = pl.ds(first + step, 1)
        coarse, fine = slice(tiles, tiles + TILE // FINE), slice(tiles + TILE // FINE, None)
        turn = turned(
            (cos_ref[start, :], sin_ref[start, :]), (cos_ref[coarse, :], sin_ref[coarse, :])
        )
        steps = cos_ref[fine, :], sin_ref[fine, :]
        for a in range(TILE // FINE):
            rows = slice(a * FINE, (a + 1) * FINE)
            cos, sin = turned([part[a : a + 1, :] for part in turn], steps)
            table[rows, :] = cos.astype(jnp.bfloat16)
            table[TILE + a * FINE : TILE + (a + 1) * FINE, :] = sin.astype(jnp.bfloat16)

    def products(prods, start, even, odd, even_level, prev, after):
        for s in range(0, count, SLAB):
            rows = slice(start + s, start + s + SLAB)

            def put(slot, receiver, source):
                rre, rim = receiver
                wre, wim = source
                to = slice(slot * count + s, slot * count + s + SLAB)
                prods[to, :TILE] = (rre * wre + rim * wim).astype(jnp.bfloat16)
                prods[to, TILE:] = (rim * wre - rre * wim).astype(jnp.bfloat16)

            even_rec, odd_rec = load(even, rows), load(odd, rows)
            even_white = whiten(even_rec, levels[rows, even_level : even_level + 1])
            prev_white = whiten(load(prev, rows), levels[rows, 2:3])
            put(0, odd_rec, even_white)
            put(1, even_rec, prev_white)
            put(2, odd_rec, prev_white)
            put(3, load(after, rows), even_white)

    def run(*blocks):
        fill_table()
        stack = None
        for part, prods in enumerate(refs):
            products(prods, part * count, *blocks)
            pairs = slice(part * 4 * count, (part + 1) * 4 * count)
            sums = jnp.dot(onehot[:, pairs], prods[...], preferred_element_type=jnp.float32)
            stack = sums if stack is None else stack + sums
        high = stack.astype(jnp.bfloat16)
        lagged = jnp.dot(high, table[...], preferred_element_type=jnp.float32)
        if first == 0:
            low = (stack - high.astype(jnp.float32)).astype(jnp.bfloat16)
            lagged += jnp.dot(low, table[...], preferred_element_type=jnp.float32)

        @pl.when(step == 0)
        def _():
            total[...] = total_in[...] + lagged if first else lagged

        @pl.when(step > 0)
        def _():
            total[...] += lagged

    pl.when(core[0] == 0)(lambda: run(own, sib, 0, from_sib, from_own))
    pl.when(core[0] != 0)(lambda: run(sib, own, 1, from_own, from_sib))

    if is_last:
        parts, rows, lags = out_ref.shape
        bands = total.shape[1] // lags

        @pl.when(step == pl.num_programs(0) - 1)
        def _():
            for part in range(parts):
                chip, f = part // bands, part % bands * lags
                for ref, owner in ((out_ref, core[0]), (give_ref, 1 - core[0])):
                    start = pl.multiple_of((2 * chip + owner) * rows, rows)
                    ref[part] = total[pl.ds(start, rows), f : f + lags]


def add_pairs(first, core, row, own, sib, from_own, from_sib, levels, phase, total, out, bins):
    cut = own.shape[2]
    pairs = row.shape[1]

    def whole(array):
        return pl.BlockSpec(array.shape, lambda t: (0,) * array.ndim)

    def columns(array):
        return pl.BlockSpec((2, array.shape[1], TILE), lambda t: (0, 0, t))

    blocks = [own, sib, from_own, from_sib]
    ins = [core, row, *blocks, levels, *phase]
    specs = [pl.BlockSpec(memory_space=pltpu.SMEM), whole(row)]
    specs += [columns(b) for b in blocks] + [whole(levels)] + [whole(p) for p in phase]
    scratch = [pltpu.VMEM((bins, pairs), jnp.bfloat16), pltpu.VMEM((2 * TILE, LAGS), jnp.bfloat16)]
    if total is not None:
        ins.append(total)
        specs.append(whole(total))
    is_last = out is not None
    if is_last:
        scratch.append(pltpu.VMEM((bins, LAGS), jnp.float32))
    else:
        out = jax.ShapeDtypeStruct((bins, LAGS), jnp.float32)
    return pl.pallas_call(
        functools.partial(pairs_kernel, first, is_last),
        grid=(cut // TILE,),
        in_specs=specs,
        out_specs=[whole(out)] * (1 + is_last),
        out_shape=[out] * (1 + is_last),
        scratch_shapes=scratch
        + [pltpu.VMEM((pairs // PARTS, 2 * TILE), jnp.bfloat16)] * PARTS,
        compiler_params=params(40),
        cost_estimate=cost(),
        name="add_pairs",
    )(*ins)


def shards(records, chan_pos, bin_row, pair_mask):
    here = lax.axis_index("chan")
    core, chip = here % 2, here // 2
    blocks, bands = lax.axis_size("chan"), lax.axis_size("freq")
    width, _, band = records.shape
    half = width // 2
    bins = bin_row.shape[0]

    core_ref = core.astype(jnp.int32)[None]
    own, give = [[block] for block in head_planes(records, core_ref, CUTS[0])]
    own_power, give_power = powers(own[0], give[0])
    sib = [to_sibling(give[0])]
    moved = [to_chips(own[0], (-1, 1)), to_chips(sib[0], (1, -1))]
    records, sib[0] = after(records, sib[0])
    (*rest_own, more_own), (*rest, more_give) = planes(
        records, core_ref, CUTS[0], CUTS[1:], True
    )
    own, own_power, give_power = own + rest_own, own_power + more_own, give_power + more_give

    totals = lax.psum(jnp.sum(jnp.stack([own_power, give_power]), axis=2), "freq")
    mask = pair_mask[0].astype(jnp.float32)
    own_info = jnp.concatenate([totals[0], mask])
    sib_info = to_sibling(jnp.concatenate([totals[1], mask]))
    own_info_moved = to_chips(own_info, (-1, 1), 1)
    sib_info_moved = to_chips(sib_info, (1, -1), 1)
    phase = phases(lax.axis_index("freq") * band, band // TILE)

    own[1], own_info_moved, phase = after(own[1], own_info_moved, phase)


    sib += [to_sibling(block) for block in rest]
    sib[1], sib_info_moved, moved[1] = after(sib[1], sib_info_moved, moved[1])
    moved += [to_chips(own[1], (-1, 1)), to_chips(sib[1], (1, -1))]

    even_mask = jnp.where(core == 0, mask, sib_info[half:])
    odd_mask = jnp.where(core == 0, sib_info[half:], mask)
    prev_info = jnp.where(core == 0, sib_info_moved, own_info_moved)
    next_info = jnp.where(core == 0, own_info_moved, sib_info_moved)

    totals = jnp.stack([own_info[:half], sib_info[:half], prev_info[:half]], axis=1)
    levels = water * totals / NF + tiny

    places = jnp.pad(chan_pos.reshape(blocks, width), ((1, 1), (0, 0)))
    places = lax.dynamic_slice(places, (2 * chip, core * half), (4, half))
    prev_pos, even_pos, odd_pos, next_pos = places
    apart = jnp.abs(
        jnp.concatenate(
            [odd_pos - even_pos, even_pos - prev_pos, odd_pos - prev_pos, next_pos - even_pos]
        )
    )
    used = jnp.stack(
        [
            odd_mask[0] > 0,
            (even_mask[0] > 0) & (chip > 0),
            (odd_mask[1] > 0) & (chip > 0),
            (next_info[half + 1] > 0) & (chip < blocks // 2 - 1),
        ]
    )
    bin_ids = jnp.arange(bins, dtype=jnp.int32)
    row = jnp.sum(jnp.where(apart[:, None] == bin_ids[None, :], bin_row[None, :], 0), axis=1)
    row = jnp.where(jnp.repeat(used, half), row, -1)
    row = row.reshape(4, PARTS, half // PARTS).transpose(1, 0, 2).reshape(-1)

    out = jax.ShapeDtypeStruct((blocks // 2 * bands, bins // blocks, LAGS // bands), jnp.float32)
    total, start = None, 0
    for k, cut in enumerate(CUTS):
        arrays = own[k], sib[k], moved[2 * k], moved[2 * k + 1]
        goal = out if k == len(CUTS) - 1 else None
        total, *give = add_pairs(
            start // TILE, core_ref, row[None, :], *arrays, levels, phase, total, goal, bins
        )
        if k + 2 < len(CUTS):
            own[k + 2], sib[k + 2], total = after(own[k + 2], sib[k + 2], total)
            moved += [to_chips(own[k + 2], (-1, 1)), to_chips(sib[k + 2], (1, -1))]
        start += cut

    total = (total + to_sibling(*give)).astype(jnp.bfloat16)
    ways = [[i * bands + f for i in range(c, blocks, 2) for f in range(bands)] for c in (0, 1)]
    parts = lax.all_to_all(
        total, ("chan", "freq"), 0, 0, axis_index_groups=ways, tiled=True
    )
    return jnp.sum(parts.astype(jnp.float32), axis=0)


def solution(mesh):
    placed = (P("chan", None, "freq"), P(), P(), P("chan", None))
    return jax.shard_map(
        shards, mesh=mesh, in_specs=placed, out_specs=P("chan", "freq"), check_vma=False
    )
```

```python
import functools
import math

import jax
import jax.numpy as jnp
from jax import lax
from jax.experimental import pallas as pl
from jax.experimental.pallas import tpu as pltpu
from jax.sharding import PartitionSpec as P

NF = 8192
LAGS = 1024

water = 0.5
tiny = 1e-06

TILE = 256
SLAB = 16
FINE = 16
LANES = 128
PARTS = 4
CUTS = (1024, 768, 256)


def params(mebibytes=57):
    return pltpu.CompilerParams(vmem_limit_bytes=mebibytes * 1024 * 1024)


def cost():
    return pl.CostEstimate(flops=1, bytes_accessed=1, transcendentals=0)


def after(*arrays):
    return lax.optimization_barrier(arrays)


def to_sibling(block):
    return lax.ppermute(block, "chan", [(i, i ^ 1) for i in range(lax.axis_size("chan"))])


def to_chips(block, core_steps, bands=0):
    devices, count = range(lax.axis_size("chan")), lax.axis_size("freq")
    route = [(i, i + 2 * core_steps[i % 2]) for i in devices]
    route = [(i, j) for i, j in route if j in devices]
    if not bands:
        return lax.ppermute(block, "chan", route)
    route = [
        (i * count + f, j * count + (f + bands) % count) for i, j in route for f in range(count)
    ]
    return lax.ppermute(block, ("chan", "freq"), route)


def phases(first, tiles):
    tile = first + TILE * jnp.arange(tiles, dtype=jnp.int32)
    coarse = FINE * jnp.arange(TILE // FINE, dtype=jnp.int32)
    freqs = jnp.concatenate([tile, coarse, jnp.arange(FINE, dtype=jnp.int32)])
    lagvec = jnp.arange(LAGS, dtype=jnp.int32) - LAGS // 2
    phase = jnp.mod(freqs[:, None] * lagvec[None, :], 2 * NF)
    theta = 2.0 * math.pi / (2 * NF) * phase.astype(jnp.float32)
    scale = jnp.where(jnp.arange(len(freqs)) < tiles, 1.0 / math.sqrt(NF), 1.0)[:, None]
    return jnp.cos(theta) * scale, -jnp.sin(theta) * scale


def turned(one, other):
    return one[0] * other[0] - one[1] * other[1], one[1] * other[0] + one[0] * other[1]


def power_of(planes):
    re, im = planes[0].astype(jnp.float32), planes[1].astype(jnp.float32)
    power = re * re + im * im
    total = power[:, :LANES]
    for f in range(LANES, power.shape[1], LANES):
        total += power[:, f : f + LANES]
    return total


def planes_kernel(with_power, core_ref, *refs):
    count = len(refs) // 2 - 1
    for n, records_ref in enumerate(refs[:2]):
        outs = refs[2 + n * count : 2 + (n + 1) * count]
        for s in range(0, records_ref.shape[0], SLAB):
            planes = jnp.swapaxes(records_ref[s : s + SLAB], 0, 1)
            start = 0
            for ref in outs[: count - with_power]:
                cut = ref.shape[2]
                ref[:, s : s + SLAB, :] = planes[:, :, start : start + cut]
                start += cut
            if with_power:
                outs[-1][s : s + SLAB, :] = power_of(planes)


def planes(records, core, start, cuts, with_power):
    half = records.shape[0] // 2
    width = sum(cuts)
    column = start // width
    block = 256
    steps = half // block
    outs = [pl.BlockSpec((2, block, cut), lambda t, c: (0, t, 0)) for cut in cuts]
    shapes = [jax.ShapeDtypeStruct((2, half, cut), jnp.bfloat16) for cut in cuts]
    if with_power:
        outs += [pl.BlockSpec((block, LANES), lambda t, c: (t, 0))]
        shapes += [jax.ShapeDtypeStruct((half, LANES), jnp.float32)]
    spec = pltpu.PrefetchScalarGridSpec(
        num_scalar_prefetch=1,
        grid=(steps,),
        in_specs=[
            pl.BlockSpec((block, 2, width), lambda t, c: (c[0] * steps + t, 0, column)),
            pl.BlockSpec((block, 2, width), lambda t, c: ((1 - c[0]) * steps + t, 0, column)),
        ],
        out_specs=outs * 2,
    )
    results = pl.pallas_call(
        functools.partial(planes_kernel, int(with_power)),
        grid_spec=spec,
        out_shape=shapes * 2,
        compiler_params=params(),
        cost_estimate=cost(),
        name="planes",
    )(core, records, records)
    return list(results[: len(outs)]), list(results[len(outs) :])


def head_kernel(core_ref, records_ref, own_ref, give_ref, raw, done, came, gone):
    _, half, width = own_ref.shape
    pieces, block = raw.shape[:2]
    per_side = pieces // 2

    def copy_in(n):
        side, row = n // per_side, n % per_side * block
        first = (core_ref[0] if side == 0 else 1 - core_ref[0]) * half + row
        rows = pl.ds(pl.multiple_of(first, block), block)
        return pltpu.make_async_copy(records_ref.at[rows, :, :width], raw.at[n], came.at[n])

    def copy_out(n):
        out_ref, row = (own_ref, give_ref)[n // per_side], n % per_side * block
        return pltpu.make_async_copy(done.at[n], out_ref.at[:, row : row + block, :], gone.at[n])

    for n in range(pieces):
        copy_in(n).start()
    for n in range(pieces):
        copy_in(n).wait()
        for s in range(0, block, SLAB):
            done[n, :, s : s + SLAB, :] = jnp.swapaxes(raw[n, s : s + SLAB], 0, 1)
        copy_out(n).start()
    for n in range(pieces):
        copy_out(n).wait()


def head_planes(records, core, width):
    half = records.shape[0] // 2
    pieces, block = 8, half // 4
    out = jax.ShapeDtypeStruct((2, half, width), jnp.bfloat16)
    return pl.pallas_call(
        head_kernel,
        in_specs=[pl.BlockSpec(memory_space=pltpu.SMEM), pl.BlockSpec(memory_space=pl.ANY)],
        out_specs=[pl.BlockSpec(memory_space=pl.ANY)] * 2,
        out_shape=[out, out],
        scratch_shapes=[
            pltpu.VMEM((pieces, block, 2, width), jnp.bfloat16),
            pltpu.VMEM((pieces, 2, block, width), jnp.bfloat16),
            pltpu.SemaphoreType.DMA((pieces,)),
            pltpu.SemaphoreType.DMA((pieces,)),
        ],
        compiler_params=params(),
        cost_estimate=cost(),
        name="head_planes",
    )(core, records)


def power_kernel(*refs):
    for planes_ref, power_ref in zip(refs[:2], refs[2:]):
        for s in range(0, planes_ref.shape[1], SLAB):
            power_ref[s : s + SLAB, :] = power_of(planes_ref[:, s : s + SLAB, :])


def powers(*blocks):
    _, channels, width = blocks[0].shape
    block = channels // 2
    out = jax.ShapeDtypeStruct((channels, LANES), jnp.float32)
    return pl.pallas_call(
        power_kernel,
        grid=(channels // block,),
        in_specs=[pl.BlockSpec((2, block, width), lambda t: (0, t, 0))] * 2,
        out_specs=[pl.BlockSpec((block, LANES), lambda t: (t, 0))] * 2,
        out_shape=[out, out],
        compiler_params=params(),
        cost_estimate=cost(),
        name="powers",
    )(*blocks)


def load(ref, rows):
    return ref[0, rows, :].astype(jnp.float32), ref[1, rows, :].astype(jnp.float32)


def whiten(spectrum, level):
    re, im = spectrum
    inverse = pltpu.reciprocal(re * re + im * im + level, approx=True)
    return (
        (re * inverse).astype(jnp.bfloat16).astype(jnp.float32),
        (im * inverse).astype(jnp.bfloat16).astype(jnp.float32),
    )


def pairs_kernel(first, is_last, core, row_ref, own, sib, from_own, from_sib, *refs):
    levels, cos_ref, sin_ref, *refs = refs
    total_in = refs.pop(0) if first else None
    out_ref, *refs = refs
    give_ref = refs.pop(0) if is_last else None
    onehot, table, *refs = refs
    total = refs.pop(0) if is_last else out_ref
    step = pl.program_id(0)
    count = own.shape[1] // len(refs)

    def fill_onehot(start, stop):
        for k in range(start, stop, 256):
            bin_row = lax.broadcasted_iota(jnp.int32, (onehot.shape[0], 256), 0)
            hit = bin_row == row_ref[:, k : k + 256]
            onehot[:, k : k + 256] = jnp.where(hit, 1.0, 0.0).astype(jnp.bfloat16)

    one_step = is_last and CUTS[-1] == TILE
    if not one_step:
        pl.when(step == 0)(lambda: fill_onehot(0, onehot.shape[1]))

    def fill_table():
        tiles = cos_ref.shape[0] - TILE // FINE - FINE
        start = pl.ds(first + step, 1)
        coarse, fine = slice(tiles, tiles + TILE // FINE), slice(tiles + TILE // FINE, None)
        turn = turned(
            (cos_ref[start, :], sin_ref[start, :]), (cos_ref[coarse, :], sin_ref[coarse, :])
        )
        steps = cos_ref[fine, :], sin_ref[fine, :]
        for a in range(TILE // FINE):
            rows = slice(a * FINE, (a + 1) * FINE)
            cos, sin = turned([part[a : a + 1, :] for part in turn], steps)
            table[rows, :] = cos.astype(jnp.bfloat16)
            table[TILE + a * FINE : TILE + (a + 1) * FINE, :] = sin.astype(jnp.bfloat16)

    def products(prods, start, even, odd, even_level, prev, after):
        for s in range(0, count, SLAB):
            rows = slice(start + s, start + s + SLAB)

            def put(slot, receiver, source):
                rre, rim = receiver
                wre, wim = source
                to = slice(slot * count + s, slot * count + s + SLAB)
                prods[to, :TILE] = (rre * wre + rim * wim).astype(jnp.bfloat16)
                prods[to, TILE:] = (rim * wre - rre * wim).astype(jnp.bfloat16)

            even_rec, odd_rec = load(even, rows), load(odd, rows)
            even_white = whiten(even_rec, levels[rows, even_level : even_level + 1])
            prev_white = whiten(load(prev, rows), levels[rows, 2:3])
            put(0, odd_rec, even_white)
            put(1, even_rec, prev_white)
            put(2, odd_rec, prev_white)
            put(3, load(after, rows), even_white)

    def run(*blocks):
        fill_table()
        stack = None
        for part, prods in enumerate(refs):
            products(prods, part * count, *blocks)
            pairs = slice(part * 4 * count, (part + 1) * 4 * count)
            if one_step:
                fill_onehot(pairs.start, pairs.stop)
            sums = jnp.dot(onehot[:, pairs], prods[...], preferred_element_type=jnp.float32)
            stack = sums if stack is None else stack + sums
        high = stack.astype(jnp.bfloat16)
        lagged = jnp.dot(high, table[...], preferred_element_type=jnp.float32)
        if first == 0:
            low = (stack - high.astype(jnp.float32)).astype(jnp.bfloat16)
            lagged += jnp.dot(low, table[...], preferred_element_type=jnp.float32)

        @pl.when(step == 0)
        def _():
            total[...] = total_in[...] + lagged if first else lagged

        @pl.when(step > 0)
        def _():
            total[...] += lagged

    pl.when(core[0] == 0)(lambda: run(own, sib, 0, from_sib, from_own))
    pl.when(core[0] != 0)(lambda: run(sib, own, 1, from_own, from_sib))

    if is_last:
        parts, rows, lags = out_ref.shape
        bands = total.shape[1] // lags

        @pl.when(step == pl.num_programs(0) - 1)
        def _():
            for part in range(parts):
                chip, f = part // bands, part % bands * lags
                for ref, owner in ((out_ref, core[0]), (give_ref, 1 - core[0])):
                    start = pl.multiple_of((2 * chip + owner) * rows, rows)
                    ref[part] = total[pl.ds(start, rows), f : f + lags]


def add_pairs(first, core, row, own, sib, from_own, from_sib, levels, phase, total, out, bins):
    cut = own.shape[2]
    pairs = row.shape[1]

    def whole(array):
        return pl.BlockSpec(array.shape, lambda t: (0,) * array.ndim)

    def columns(array):
        return pl.BlockSpec((2, array.shape[1], TILE), lambda t: (0, 0, t))

    blocks = [own, sib, from_own, from_sib]
    ins = [core, row, *blocks, levels, *phase]
    specs = [pl.BlockSpec(memory_space=pltpu.SMEM), whole(row)]
    specs += [columns(b) for b in blocks] + [whole(levels)] + [whole(p) for p in phase]
    scratch = [pltpu.VMEM((bins, pairs), jnp.bfloat16), pltpu.VMEM((2 * TILE, LAGS), jnp.bfloat16)]
    if total is not None:
        ins.append(total)
        specs.append(whole(total))
    is_last = out is not None
    if is_last:
        scratch.append(pltpu.VMEM((bins, LAGS), jnp.float32))
    else:
        out = jax.ShapeDtypeStruct((bins, LAGS), jnp.float32)
    return pl.pallas_call(
        functools.partial(pairs_kernel, first, is_last),
        grid=(cut // TILE,),
        in_specs=specs,
        out_specs=[whole(out)] * (1 + is_last),
        out_shape=[out] * (1 + is_last),
        scratch_shapes=scratch
        + [pltpu.VMEM((pairs // PARTS, 2 * TILE), jnp.bfloat16)] * PARTS,
        compiler_params=params(40),
        cost_estimate=cost(),
        name="add_pairs",
    )(*ins)


def shards(records, chan_pos, bin_row, pair_mask):
    here = lax.axis_index("chan")
    core, chip = here % 2, here // 2
    blocks, bands = lax.axis_size("chan"), lax.axis_size("freq")
    width, _, band = records.shape
    half = width // 2
    bins = bin_row.shape[0]

    core_ref = core.astype(jnp.int32)[None]
    own, give = [[block] for block in head_planes(records, core_ref, CUTS[0])]
    own_power, give_power = powers(own[0], give[0])
    sib = [to_sibling(give[0])]
    moved = [to_chips(own[0], (-1, 1)), to_chips(sib[0], (1, -1))]
    records, sib[0] = after(records, sib[0])
    (*rest_own, more_own), (*rest, more_give) = planes(
        records, core_ref, CUTS[0], CUTS[1:], True
    )
    own, own_power, give_power = own + rest_own, own_power + more_own, give_power + more_give

    totals = lax.psum(jnp.sum(jnp.stack([own_power, give_power]), axis=2), "freq")
    mask = pair_mask[0].astype(jnp.float32)
    own_info = jnp.concatenate([totals[0], mask])
    sib_info = to_sibling(jnp.concatenate([totals[1], mask]))
    own_info_moved = to_chips(own_info, (-1, 1), 1)
    sib_info_moved = to_chips(sib_info, (1, -1), 1)
    phase = phases(lax.axis_index("freq") * band, band // TILE)

    own[1], own_info_moved, phase = after(own[1], own_info_moved, phase)


    sib += [to_sibling(block) for block in rest]
    sib[1], sib_info_moved, moved[1] = after(sib[1], sib_info_moved, moved[1])
    moved += [to_chips(own[1], (-1, 1)), to_chips(sib[1], (1, -1))]

    even_mask = jnp.where(core == 0, mask, sib_info[half:])
    odd_mask = jnp.where(core == 0, sib_info[half:], mask)
    prev_info = jnp.where(core == 0, sib_info_moved, own_info_moved)
    next_info = jnp.where(core == 0, own_info_moved, sib_info_moved)

    totals = jnp.stack([own_info[:half], sib_info[:half], prev_info[:half]], axis=1)
    levels = water * totals / NF + tiny

    places = jnp.pad(chan_pos.reshape(blocks, width), ((1, 1), (0, 0)))
    places = lax.dynamic_slice(places, (2 * chip, core * half), (4, half))
    prev_pos, even_pos, odd_pos, next_pos = places
    apart = jnp.abs(
        jnp.concatenate(
            [odd_pos - even_pos, even_pos - prev_pos, odd_pos - prev_pos, next_pos - even_pos]
        )
    )
    used = jnp.stack(
        [
            odd_mask[0] > 0,
            (even_mask[0] > 0) & (chip > 0),
            (odd_mask[1] > 0) & (chip > 0),
            (next_info[half + 1] > 0) & (chip < blocks // 2 - 1),
        ]
    )
    bin_ids = jnp.arange(bins, dtype=jnp.int32)
    row = jnp.sum(jnp.where(apart[:, None] == bin_ids[None, :], bin_row[None, :], 0), axis=1)
    row = jnp.where(jnp.repeat(used, half), row, -1)
    row = row.reshape(4, PARTS, half // PARTS).transpose(1, 0, 2).reshape(-1)

    out = jax.ShapeDtypeStruct((blocks // 2 * bands, bins // blocks, LAGS // bands), jnp.float32)
    total, start = None, 0
    for k, cut in enumerate(CUTS):
        arrays = own[k], sib[k], moved[2 * k], moved[2 * k + 1]
        goal = out if k == len(CUTS) - 1 else None
        total, *give = add_pairs(
            start // TILE, core_ref, row[None, :], *arrays, levels, phase, total, goal, bins
        )
        if k + 2 < len(CUTS):
            own[k + 2], sib[k + 2], total = after(own[k + 2], sib[k + 2], total)
            moved += [to_chips(own[k + 2], (-1, 1)), to_chips(sib[k + 2], (1, -1))]
        start += cut

    total = (total + to_sibling(*give)).astype(jnp.bfloat16)
    ways = [[i * bands + f for i in range(c, blocks, 2) for f in range(bands)] for c in (0, 1)]
    parts = lax.all_to_all(
        total, ("chan", "freq"), 0, 0, axis_index_groups=ways, tiled=True
    )
    return jnp.sum(parts.astype(jnp.float32), axis=0)


def solution(mesh):
    placed = (P("chan", None, "freq"), P(), P(), P("chan", None))
    return jax.shard_map(
        shards, mesh=mesh, in_specs=placed, out_specs=P("chan", "freq"), check_vma=False
    )
```
